512 devices in a mesh: emb: 16 (over x_lo, z), dp: 8 (over y), tp: 4 (over x_hi, core).
Axes of the slice: x: 4 (x_hi: 2, x_lo: 2; x = x_hi * 2 + x_lo), y: 8, z: 8, core: 2. Of those that a mesh axis runs over, the one named last changes fastest.
Arguments:
- emb_table: float32 [16384, 128], P('emb'), may hold values from -3 to 3
- row_accum: float32 [16384, 128], P('emb'), may hold values from 0.01 to 1
- dense_input: bfloat16 [32768, 128], P(('emb', 'dp')), may hold values from -6 to 6
- row_shard: int32 [32768, 52, 1], P(('emb', 'dp', 'tp')), may hold values from 0 to 15; in each aligned block of 3328 rows (0 to 3327, 3328 to 6655, ..., all dimensions but the last counted through in order) at most 312 rows name the same one
- local_row: int32 [32768, 52], P(('emb', 'dp', 'tp')), may hold values from 0 to 1023
- bag_length: int32 [32768, 13], P(('emb', 'dp', 'tp')), may hold values from 1 to 4
- labels: int32 [32768], P(('emb', 'dp')), may hold values 0 or 1
- feedback: float32 [32768, 1664], P(('emb', 'dp', 'tp')), may hold values from -0.3125 to 0.3125
- cross_down: bfloat16 [1792, 512], P(None, 'tp'), may hold values from -0.125 to 0.125
- cross_up: bfloat16 [512, 1792], P('tp'), may hold values from -0.25 to 0.25
- cross_bias: float32 [1792], replicated, may hold values from -3 to 3
- head_weight: float32 [1792], replicated, may hold values from -0.125 to 0.125
Outputs:
- table_new: float32 [16384, 128], P('emb')
- accum_new: float32 [16384, 128], P('emb')
- carried_new: float32 [32768, 1664], P(('emb', 'dp', 'tp'))
- grad_down: float32 [1792, 512], P(('emb', 'dp'), 'tp')
- grad_up: float32 [512, 1792], P('tp', ('emb', 'dp'))
- grad_bias: float32 [1792], P(('emb', 'dp'))
- grad_head: float32 [1792], P(('emb', 'dp'))
The draws below stay inside these ranges and needn't reach their ends.
Inputs may be any that keep to these rules, and one draw needn't show every extreme that they name: `row_shard`: within the 3328 lookup slots of one device (aligned blocks of samples), no shard is named by more than 312 slots, a bound that some block reaches in each draw.
All inputs are finite; a program needn't handle non-finite values. No bound on the sum of `labels` on one device may be relied on, other than what follows from the above.
Results may differ from the reference program's by a relative error of at most 0.0068.
Values may be sent and summed in bfloat16 or wider, within the bound.
No kernel may reach another device: no remote copies, remote signals or barrier semaphores. Data moves between devices by JAX's collectives and lax.ppermute only.
A program may use at most 64 MiB of HBM per device.

```python
import math
import jax
import jax.numpy as jnp
import numpy as np
from jax import lax

E = 128
F = 13
R = 512
BAG = 4
SAMP_DEV = 64
ROWS_DEV = 1024
LOOK = 52
DX = 1792
CAP = 312
BATCH = 32768
ROWS = 16384
DENSE_SAMPLES = 256
N_EMB = 16


def plant(entries, own_key, low, largest):
    longest = entries.shape.index(max(entries.shape))
    spots = []
    for shift in (0, 1):
        where = [jax.random.randint(jax.random.fold_in(own_key, axis), (), 0, length) for axis, length in enumerate(entries.shape)]
        where[longest] = (where[longest] + shift) % entries.shape[longest]
        spots.append(tuple(where))
    return entries.at[spots[0]].set(low).at[spots[1]].set(largest)


def levels(key, dims, split, low, top_value):
    factor_of, own = 1.0, jax.random.fold_in(key, 6)
    for dim, parts in split:
        heights = jnp.exp(jax.random.uniform(jax.random.fold_in(own, dim), (parts,), jnp.float32, low / len(split), top_value / len(split)))
        factor_of = factor_of * jnp.repeat(heights, dims[dim] // parts).reshape([-1 if axis == dim else 1 for axis in range(len(dims))])
    return factor_of


def rank_bounds(amount, lean):
    portions = [(1 << 20) // math.isqrt(rank ** lean) + 1 for rank in range(1, amount + 1)]
    scale = 1 + sum(portions) // (1 << 30)
    return np.cumsum(np.array([max(1, weight // scale) for weight in portions]))


def skewed_ids(stream_key, dims, count, skew):
    listing = rank_bounds(count, skew)
    pick = jax.random.randint(jax.random.fold_in(stream_key, 1), dims, 0, int(listing[count - 1]))
    rank = jnp.searchsorted(jnp.asarray(listing, jnp.int32), pick, side="right")
    return jax.random.permutation(jax.random.fold_in(stream_key, 2), count)[rank].astype(jnp.int32)


def deal_out(stream_key, own, number, rows, number_of, top, limit, skew):
    order = jax.random.permutation(stream_key, number_of)
    crowded, usual = load_shares(number_of, rows * top, limit, skew, True), load_shares(number_of, rows * top, limit, skew, False)
    places = jnp.arange(number_of)

    def named(sizes, rotation):
        used = int((sizes > 0).sum())
        fixed = max(1, used // 4)
        moved = fixed + (places - fixed + rotation * (used - fixed)) % max(1, number_of - fixed)
        return jnp.zeros((number_of,), jnp.int32).at[order[jnp.where(places < fixed, places, moved)]].set(jnp.asarray(sizes, jnp.int32))

    sizes = jnp.where(number % 4 == 0, named(crowded, number // 4), named(usual, number - number // 4 - 1))
    mixed = jax.random.permutation(jax.random.fold_in(own, 3), number_of)
    donor, receiver = mixed[0:number_of // 2 * 2:2], mixed[1:number_of // 2 * 2:2]
    room = jnp.minimum(sizes[donor] - 1, limit - sizes[receiver]) // 2
    room = jnp.where((donor == order[0]) | (receiver == order[0]) | (sizes[receiver] == 0), 0, jnp.maximum(room, 0))
    moved = jax.random.randint(jax.random.fold_in(own, 4), (number_of // 2,), 0, 1 << 20) % (room + 1)
    sizes = sizes.at[donor].add(-moved).at[receiver].add(moved)
    items = jnp.searchsorted(jnp.cumsum(sizes), jnp.arange(rows * top), side="right").astype(jnp.int32)
    listing = items.reshape(top, rows).T
    listing = listing[jax.random.permutation(jax.random.fold_in(own, 1), rows)]
    rotation = jax.random.randint(jax.random.fold_in(own, 2), (rows, 1), 0, top)
    return jnp.take_along_axis(listing, (jnp.arange(top)[None, :] + rotation) % top, axis=1)


def load_shares(number_of, total, bound, skew, full):
    loads = [(1 << 20) // math.isqrt(standing ** skew) + 1 for standing in range(1, number_of + 1)]
    largest = bound if full else min(bound, max(-(-total // number_of), total * loads[0] // sum(loads)))
    least = 1 if total - largest >= number_of - 1 else 0
    holding, surplus = [largest] + [least] * (number_of - 1), total - largest - least * (number_of - 1)
    while surplus > 0:
        candidates = [i for i in range(1, number_of) if holding[i] < largest] or [i for i in range(1, number_of) if holding[i] < bound]
        whole, left = sum([loads[i] for i in candidates]), surplus
        for i in candidates:
            more = min(bound - holding[i], max(1, left * loads[i] // whole), surplus)
            holding[i] = holding[i] + more
            surplus = surplus - more
    return np.array(holding)


def noise(own_key, dims, deviation, bound, pieces=(), held_as=jnp.bfloat16):
    result = jax.random.normal(own_key, dims, jnp.float32) * deviation
    if len(pieces) > 0:
        result = levels(own_key, dims, pieces, -0.22, 0.18) * result
    return jnp.clip(result, min=-bound, max=bound).astype(held_as)


def setup_inputs(seed: int = 0) -> dict:
    key_list = jax.random.split(jax.random.key(seed), 13)
    emb_table = noise(key_list[0], (ROWS, E), 0.5, 3.0, ((0, 16),), jnp.float32)
    row_accum = jnp.clip(jnp.exp(math.log(1.0) - 4.6051702 * jax.random.uniform(key_list[1], (ROWS, E), jnp.float32) ** levels(key_list[1], (ROWS, E), ((0, 16),), -0.2, 0.2)), 0.01, 1.0)
    dense_input = noise(key_list[2], (BATCH, E), 1.0, 6.0, ((0, 128),))
    row_shard_keys = jax.random.split(jax.random.fold_in(key_list[3], 1), BATCH * LOOK // (SAMP_DEV * LOOK))
    row_shard_turns = jax.random.permutation(jax.random.fold_in(key_list[3], 3), BATCH * LOOK // (SAMP_DEV * LOOK))
    row_shard = jax.vmap(lambda own, number: deal_out(jax.random.fold_in(key_list[3], 2), own, number, SAMP_DEV * LOOK, N_EMB, 1, CAP, 2))(row_shard_keys, row_shard_turns).reshape((BATCH, LOOK, 1))
    local_row = plant(skewed_ids(key_list[4], (BATCH, LOOK), ROWS_DEV, 2), jax.random.fold_in(key_list[4], 3), 0, ROWS_DEV - 1).astype(jnp.int32)
    bag_length = plant(jax.random.randint(key_list[5], (BATCH, F), 1, BAG + 1), jax.random.fold_in(key_list[5], 1), 1, BAG).astype(jnp.int32)
    labels = plant((jax.random.randint(key_list[6], (BATCH,), 0, 2) < 1).astype(jnp.int32), jax.random.fold_in(key_list[6], 1), 0, 1)
    feedback = noise(key_list[7], (BATCH, F * E), 0.02, 0.3125, ((0, 512),), jnp.float32)
    cross_down = noise(key_list[8], (DX, R), DX ** -0.5, 0.125, ((1, 4),))
    cross_up = noise(key_list[9], (R, DX), R ** -0.5, 0.25, ((0, 4),))
    cross_bias = noise(key_list[10], (DX,), 0.5, 3.0, (), jnp.float32)
    head_weight = noise(key_list[11], (DX,), DX ** -0.5, 0.125, (), jnp.float32)
    return {"emb_table": emb_table, "row_accum": row_accum, "dense_input": dense_input, "row_shard": row_shard, "local_row": local_row, "bag_length": bag_length, "labels": labels, "feedback": feedback, "cross_down": cross_down, "cross_up": cross_up, "cross_bias": cross_bias, "head_weight": head_weight}


learn_rate = 0.5

def reference(emb_table, row_accum, dense_input, row_shard, local_row, bag_length, labels, feedback, cross_down, cross_up, cross_bias, head_weight):
    blocks = BATCH // DENSE_SAMPLES
    shard_blk = row_shard.reshape(blocks, DENSE_SAMPLES, LOOK)
    local_blk = local_row.reshape(blocks, DENSE_SAMPLES, LOOK)
    length_blk = bag_length.reshape(blocks, DENSE_SAMPLES, F)
    dense_blk = dense_input.reshape(blocks, DENSE_SAMPLES, E)
    label_blk = labels.reshape(blocks, DENSE_SAMPLES)
    carry_blk = feedback.reshape(blocks, DENSE_SAMPLES, F * E)
    embedding_down = cross_down[E:, :]

    def step(carry, block):
        grad_down, grad_up, grad_bias, grad_head, row_grad = carry
        shard_ids, local_ids, lengths, dense_rows, label_rows, carried_in = block
        row_ids = (shard_ids * ROWS_DEV + local_ids).reshape(-1)
        fetched = lax.optimization_barrier(jnp.take(emb_table, row_ids, axis=0).astype(jnp.bfloat16))
        usable = (jnp.arange(BAG, dtype=jnp.int32)[None, None, :] < lengths[:, :, None]).astype(jnp.float32)
        pooled = lax.optimization_barrier(jnp.sum(fetched.astype(jnp.float32).reshape(DENSE_SAMPLES, F, BAG, E) * usable[..., None], axis=2))
        pooled = pooled.astype(jnp.bfloat16).reshape(DENSE_SAMPLES, F * E)
        x_first = jnp.concatenate([dense_rows, pooled], axis=1)
        hidden_activation = jnp.dot(x_first, cross_down, preferred_element_type=jnp.float32).astype(jnp.bfloat16)
        crossed = jnp.dot(hidden_activation, cross_up, preferred_element_type=jnp.float32)
        x_float = x_first.astype(jnp.float32)
        x_next = x_float * (crossed + cross_bias[None, :]) + x_float
        logits = lax.optimization_barrier(jnp.sum(x_next * head_weight[None, :], axis=1))
        grad_logit = jax.nn.sigmoid(logits) - label_rows.astype(jnp.float32)
        grad_next = grad_logit[:, None] * head_weight[None, :]
        grad_cross = (grad_next * x_float).astype(jnp.bfloat16)
        hidden_gradient = lax.dot_general(grad_cross, cross_up, (((1,), (1,)), ((), ())), preferred_element_type=jnp.float32).astype(jnp.bfloat16)
        back_term = lax.dot_general(hidden_gradient, embedding_down, (((1,), (1,)), ((), ())), preferred_element_type=jnp.float32)
        grad_pool = grad_next[:, E:] * (crossed[:, E:] + cross_bias[None, E:] + 1.0) + back_term
        carried = grad_pool + carried_in
        sent = lax.optimization_barrier(carried.astype(jnp.bfloat16))
        lookup_grad = sent.astype(jnp.float32).reshape(DENSE_SAMPLES, F, 1, E) * usable[..., None]
        row_grad = row_grad.at[row_ids].add(lookup_grad.reshape(-1, E))
        grad_down = grad_down + lax.dot_general(x_first, hidden_gradient, (((0,), (0,)), ((), ())), preferred_element_type=jnp.float32)
        grad_up = grad_up + lax.dot_general(hidden_activation, grad_cross, (((0,), (0,)), ((), ())), preferred_element_type=jnp.float32)
        grad_bias = grad_bias + lax.optimization_barrier(jnp.sum(grad_next * x_float, axis=0))
        grad_head = grad_head + lax.optimization_barrier(jnp.sum(grad_logit[:, None] * x_next, axis=0))
        return ((grad_down, grad_up, grad_bias, grad_head, row_grad), carried)
    start = (jnp.zeros((DX, R), jnp.float32), jnp.zeros((R, DX), jnp.float32), jnp.zeros((DX,), jnp.float32), jnp.zeros((DX,), jnp.float32), jnp.zeros((ROWS, E), jnp.float32))
    final, carried_all = lax.scan(step, start, (shard_blk, local_blk, length_blk, dense_blk, label_blk, carry_blk))
    grad_down, grad_up, grad_bias, grad_head, row_grad = final
    accum_new = row_accum + row_grad * row_grad
    table_new = emb_table - learn_rate * row_grad / jnp.sqrt(accum_new)
    return (table_new, accum_new, carried_all.reshape(BATCH, F * E), grad_down, grad_up, grad_bias, grad_head)
```

```python
import jax
import jax.numpy as jnp
from jax import lax
from jax.experimental import pallas as pl
from jax.experimental.pallas import tpu as pltpu
from jax.sharding import Mesh, PartitionSpec as P

BF = jnp.bfloat16
F32 = jnp.float32
I32 = jnp.int32
E = 128
F = 13
BAG = 4
LOOK = F * BAG
N = 64
DENSE = 256
TP = 4
DP = 8
SHARDS = 16
CAP = 312
ROWS = 1024
DX = 1792
POOL = F * E
RANK = 128
GROUP = 14
CHUNK = 32
BAGS = N * F
LEARN = 0.5
EMB = ("xl", "z")
TPA = ("xh", "core")

VMEM = pl.BlockSpec(memory_space=pltpu.VMEM)
SMEM = pl.BlockSpec(memory_space=pltpu.SMEM)


def iota(shape, axis):
    return lax.broadcasted_iota(I32, shape, axis)


def dot(a, b, ca=1, cb=0):
    return lax.dot_general(a, b, (((ca,), (cb,)), ((), ())), preferred_element_type=F32)


def call(kernel, outs, ins, name, scratch=(), limit=40, flops=0):
    nbytes = sum(x.size * x.dtype.itemsize for x in ins)
    return pl.pallas_call(
        kernel,
        out_shape=outs,
        in_specs=[SMEM if x.size < 8 else VMEM for x in ins],
        out_specs=jax.tree.map(lambda _: VMEM, outs),
        scratch_shapes=scratch,
        compiler_params=pltpu.CompilerParams(vmem_limit_bytes=limit << 20),
        cost_estimate=pl.CostEstimate(flops=flops, bytes_accessed=nbytes, transcendentals=0),
        name=name,
    )(*ins)


def index_kernel(shard_ref, row_ref, len_ref, ids_ref, src_ref, src_t_ref):
    def spread(values):
        parts = []
        for j in range(BAG):
            pick = (iota((F, LOOK), 1) == BAG * iota((F, LOOK), 0) + j).astype(F32).astype(BF)
            parts.append(dot(pick, values.astype(F32).astype(BF), 1, 1))
        return jnp.concatenate(parts, axis=1)

    shard = spread(shard_ref[...])
    rows = row_ref[...]
    row_lo, row_hi = spread(rows & 255), spread(rows >> 8)
    eye = (iota((F, F), 0) == iota((F, F), 1)).astype(F32).astype(BF)
    lens = dot(eye, len_ref[...].astype(F32).astype(BF), 1, 1)
    lens = jnp.concatenate([lens] * BAG, axis=1)
    wide = (F, BAG * N)
    lane = iota(wide, 1)
    usable = (lane >> 6).astype(F32) < lens
    bag = jnp.where(usable, iota(wide, 0) * N + (lane & (N - 1)) + 1, 0)
    bag_lo, bag_hi = (bag & 255).astype(F32), (bag & ~255).astype(F32)
    row_hi = row_hi * 256.0

    sq = (BAG * N, BAG * N)
    upper = (iota(sq, 0) < iota(sq, 1)).astype(F32).astype(BF)
    shards = iota((SHARDS, BAG * N), 0).astype(F32)
    slots = iota((CAP, BAG * N), 0).astype(F32)
    base = jnp.zeros((SHARDS, 1), F32)
    ids = jnp.zeros((SHARDS, CAP), F32)
    src = jnp.zeros((SHARDS, CAP), F32)
    src_t = jnp.zeros((CAP, SHARDS), F32)
    for f in range(F):
        hit = shards == shard[f : f + 1, :]
        one = jnp.where(hit, 1.0, 0.0)
        before = dot(one.astype(BF), upper) + base
        base = base + jnp.sum(one, axis=1, keepdims=True)
        rank = jnp.sum(one * before, axis=0, keepdims=True)
        place = jnp.where(slots == rank, 1.0, 0.0).astype(BF)

        def put(v):
            return jnp.where(hit, v[f : f + 1, :], 0.0).astype(BF)

        lo, hi = put(bag_lo), put(bag_hi)
        ids = ids + dot(put(row_lo), place, 1, 1) + dot(put(row_hi), place, 1, 1)
        src = src + dot(lo, place, 1, 1) + dot(hi, place, 1, 1)
        src_t = src_t + dot(place, lo, 1, 1) + dot(place, hi, 1, 1)
    ids_ref[...] = ids.astype(I32)
    src_ref[...] = src.astype(I32) - 1
    src_t_ref[...] = src_t.astype(I32) - 1


def fetch_kernel(ids_ref, table_ref, out_ref):
    table = table_ref[...].astype(BF)
    cols = jnp.transpose(ids_ref[...].astype(F32))
    lanes = iota((CAP, ROWS), 1).astype(F32)
    for s in range(SHARDS):
        pick = jnp.where(cols[:, s : s + 1] == lanes, 1.0, 0.0).astype(BF)
        out_ref[s] = dot(pick, table).astype(BF)


def pool_kernel(rows_ref, src_ref, out_ref, acc_ref):
    bags = iota((BAGS, CAP), 0)
    for s in range(SHARDS):
        pick = jnp.where(bags == src_ref[s : s + 1, :], 1.0, 0.0).astype(BF)
        term = dot(pick, rows_ref[s])
        if s == 0:
            acc_ref[...] = term
        else:
            acc_ref[...] += term
    for f in range(F):
        out_ref[:, f * E : (f + 1) * E] = acc_ref[f * N : (f + 1) * N, :].astype(BF)


def dense_kernel(
    where_ref, pooled_ref, dense_ref, down_ref, up_ref, bias_ref, head_ref, label_ref,
    feedback_ref, src_t_ref, carried_ref, send_ref, small_ref,
):
    first = pl.multiple_of(where_ref[0] * N, N)
    x = jnp.concatenate([dense_ref[pl.ds(first, N), :], pooled_ref[...]], axis=1)
    hidden = jnp.concatenate([dot(x, down_ref[k]).astype(BF) for k in range(TP)], axis=1)
    up = up_ref[...]
    crossed = dot(hidden, up)
    xf = x.astype(F32)
    bias, head = bias_ref[...], head_ref[...]
    x_next = xf * (crossed + bias) + xf
    logits = jnp.sum(x_next * head, axis=1, keepdims=True)
    grad_logit = jax.nn.sigmoid(logits) - label_ref[pl.ds(first, N), :].astype(F32)
    grad_next = grad_logit * head
    grad_cross = (grad_next * xf).astype(BF)
    grad_hidden = dot(grad_cross, up, 1, 1).astype(BF)
    back = dot(grad_hidden[:, :RANK], down_ref[0][E:, :], 1, 1)
    for k in range(1, TP):
        back = back + dot(grad_hidden[:, k * RANK : (k + 1) * RANK], down_ref[k][E:, :], 1, 1)
    carried = grad_next[:, E:] * (crossed[:, E:] + bias[:, E:] + 1.0) + back + feedback_ref[...]
    carried_ref[...] = carried
    sent = carried.astype(BF)
    by_bag = jnp.concatenate([sent[:, f * E : (f + 1) * E] for f in range(F)], axis=0)
    bags = iota((CAP, BAGS), 1)
    for s in range(SHARDS):
        pick = jnp.where(src_t_ref[:, s : s + 1] == bags, 1.0, 0.0).astype(BF)
        send_ref[s] = dot(pick, by_bag).astype(BF)
    small_ref[0:N, :] = jnp.broadcast_to(grad_logit, (N, E))
    grad_head = jnp.sum(grad_logit * x_next, axis=0, keepdims=True)
    for j in range(DX // E):
        small_ref[N + j : N + j + 1, :] = grad_head[:, j * E : (j + 1) * E]
    small_ref[N + DX // E :, :] = jnp.zeros((2, E), F32)


def grads_kernel(
    where_ref, pooled_ref, dense_ref, down_ref, up_ref, head_ref, s0_ref, s1_ref, s2_ref, s3_ref,
    *rest,
):
    outs, (logit_ref, down_grad_ref, up_grad_ref, stage_ref) = rest[:DP], rest[DP:]
    t, y = where_ref[0], where_ref[1]
    for m, ref in enumerate((s0_ref, s1_ref, s2_ref, s3_ref)):
        logit_ref[pl.ds(pl.multiple_of((t ^ m) * N, N), N), :] = ref[0:N, :]
    x = jnp.concatenate([dense_ref[...], pooled_ref[...]], axis=1)
    xf = x.astype(F32)
    hidden = dot(x, down_ref[...]).astype(BF)
    cross = logit_ref[:, 0:1] * head_ref[...] * xf
    grad_bias = jnp.sum(cross, axis=0, keepdims=True)
    grad_cross = cross.astype(BF)
    grad_hidden = dot(grad_cross, up_ref[...], 1, 1).astype(BF)
    down_grad_ref[...] = dot(x, grad_hidden, 0, 0).astype(BF)
    up_grad_ref[...] = dot(grad_cross, hidden, 0, 0).astype(BF)

    tail = slice(N, N + DX // E)
    heads = (s0_ref[tail, :] + s1_ref[tail, :]) + (s2_ref[tail, :] + s3_ref[tail, :])
    grad_head = jnp.concatenate([heads[j : j + 1, :] for j in range(DX // E)], axis=1)
    groups = DX // GROUP
    r = iota((groups, DX), 1) - GROUP * iota((groups, DX), 0)
    own = (r >= 0) & (r < GROUP)
    rows = iota((DX, E), 0)
    rest14 = rows - GROUP * jnp.floor((rows.astype(F32) + 0.5) * (1.0 / GROUP)).astype(I32)
    small = jnp.zeros((groups, E), F32)
    for p, v in enumerate((grad_head, grad_bias)):
        spread = jnp.where(own, v, 0.0).astype(BF)
        lanes = jnp.where(iota((DX, E), 1) == rest14 + 16 * p, 1.0, 0.0).astype(BF)
        small = small + dot(spread, lanes)

    block = DP * GROUP
    q = (DP * CHUNK, 2 * block + 32)
    d, rho, col = iota(q, 0) >> 5, iota(q, 0) & 31, iota(q, 1)
    want = jnp.where(
        rho < GROUP,
        GROUP * d + rho,
        jnp.where(
            rho < 2 * GROUP,
            block + GROUP * d + rho - GROUP,
            jnp.where(rho == 2 * GROUP, 2 * block + d, -1),
        ),
    )
    select = jnp.where(col == want, 1.0, 0.0).astype(BF)
    for e in range(SHARDS):
        part = jnp.concatenate([small[DP * e : DP * e + DP], jnp.zeros((24, E), F32)], axis=0)
        block_rows = jnp.concatenate(
            [
                down_grad_ref[block * e : block * (e + 1), :],
                up_grad_ref[block * e : block * (e + 1), :],
                part.astype(BF),
            ],
            axis=0,
        )
        got = dot(select, block_rows).astype(BF)
        for k in range(DP):
            stage_ref[k, e] = got[CHUNK * k : CHUNK * (k + 1)]
    for s in range(DP):
        outs[s][...] = stage_ref[(y + s) & (DP - 1)]


def scatter_kernel(ids_ref, rows_ref, out_ref, acc_ref):
    rows = iota((ROWS, CAP), 0)
    for s in range(SHARDS):
        pick = jnp.where(rows == ids_ref[s : s + 1, :], 1.0, 0.0).astype(BF)
        term = dot(pick, rows_ref[s])
        if s == 0:
            acc_ref[...] = term
        else:
            acc_ref[...] += term
    out_ref[...] = acc_ref[...].astype(BF)


def total(parts):
    parts = [p.astype(F32) for p in parts]
    while len(parts) > 1:
        parts = [a + b for a, b in zip(parts[::2], parts[1::2])]
    return parts[0]


def sds(shape, dtype):
    return jax.ShapeDtypeStruct(shape, dtype)


def local(
    emb_table, row_accum, dense_input, row_shard, local_row, bag_length, labels, feedback,
    cross_down, cross_up, cross_bias, head_weight,
):
    bias, head = cross_bias.reshape(1, DX), head_weight.reshape(1, DX)
    where = jnp.stack([lax.axis_index(TPA), lax.axis_index("y")]).astype(I32)
    with jax.named_scope("gather_weights"):
        down_all = lax.all_gather(cross_down, TPA, axis=0, tiled=False)
        up_all = lax.all_gather(cross_up, TPA, axis=0, tiled=True)
    ids, src, src_t = call(
        index_kernel,
        (sds((SHARDS, CAP), I32), sds((SHARDS, CAP), I32), sds((CAP, SHARDS), I32)),
        (row_shard.reshape(N, LOOK), local_row, bag_length),
        "index",
        flops=400_000_000,
    )
    ids = lax.all_to_all(ids, EMB, split_axis=0, concat_axis=0, tiled=True)
    fetched = call(
        fetch_kernel, sds((SHARDS, CAP, E), BF), (ids, emb_table), "fetch", flops=1_300_000_000
    )
    returned = lax.all_to_all(fetched, EMB, split_axis=0, concat_axis=0, tiled=True)
    pooled = call(
        pool_kernel,
        sds((N, POOL), BF),
        (returned, src),
        "pool",
        scratch=[pltpu.VMEM((BAGS, E), F32)],
        flops=1_060_000_000,
    )
    pooled_all = lax.all_gather(pooled, TPA, axis=0, tiled=True)
    carried, send, small = call(
        dense_kernel,
        (sds((N, POOL), F32), sds((SHARDS, CAP, E), BF), sds((N + 16, E), F32)),
        (where, pooled, dense_input, down_all, up_all, bias, head, labels.reshape(DENSE, 1), feedback, src_t),
        "dense",
        flops=1_500_000_000,
    )
    arrived = lax.all_to_all(send, EMB, split_axis=0, concat_axis=0, tiled=True)

    swap = [(0, 1), (1, 0)]
    cross4 = [(i, i ^ 3) for i in range(TP)]
    s1 = lax.ppermute(small, "core", swap)
    s2 = lax.ppermute(small, "xh", swap)
    s3 = lax.ppermute(small, TPA, cross4)
    outs = call(
        grads_kernel,
        [sds((SHARDS, CHUNK, E), BF)] * DP,
        (where, pooled_all, dense_input, cross_down, cross_up, head, small, s1, s2, s3),
        "grads",
        scratch=[
            pltpu.VMEM((DENSE, E), F32),
            pltpu.VMEM((DX, RANK), BF),
            pltpu.VMEM((DX, RANK), BF),
            pltpu.VMEM((DP, SHARDS, CHUNK, E), BF),
        ],
        flops=1_000_000_000,
    )
    pieces = [outs[0]]
    for s in range(1, DP):
        pieces.append(lax.ppermute(outs[s], "y", [(i, (i + s) % DP) for i in range(DP)]))
    over_y = total(pieces).astype(BF)
    over_all = lax.all_to_all(over_y, EMB, split_axis=0, concat_axis=0, tiled=True)
    grads = jnp.sum(over_all.astype(F32), axis=0)
    grad_down = grads[0:GROUP]
    grad_up = grads[GROUP : 2 * GROUP].T
    grad_head = grads[2 * GROUP, 0:GROUP]
    grad_bias = grads[2 * GROUP, 16 : 16 + GROUP]

    row_grad = call(
        scatter_kernel,
        sds((ROWS, E), BF),
        (ids, arrived),
        "scatter",
        scratch=[pltpu.VMEM((ROWS, E), F32)],
        flops=1_300_000_000,
    )
    by_y = lax.all_to_all(row_grad, "y", split_axis=0, concat_axis=0, tiled=True)
    mine = jnp.sum(by_y.reshape(DP, ROWS // DP, E).astype(F32), axis=0).astype(BF)
    m1 = lax.ppermute(mine, "core", swap)
    m2 = lax.ppermute(mine, "xh", swap)
    m3 = lax.ppermute(mine, TPA, cross4)
    mine = total([mine, m1, m2, m3]).astype(BF)
    spread = jnp.broadcast_to(mine[None], (DP, ROWS // DP, E)).reshape(ROWS, E)
    full = lax.all_to_all(spread, "y", split_axis=0, concat_axis=0, tiled=True).astype(F32)
    accum_new = row_accum + full * full
    table_new = emb_table - LEARN * full / jnp.sqrt(accum_new)
    return (table_new, accum_new, carried, grad_down, grad_up, grad_bias, grad_head)


def solution(mesh):
    fine = Mesh(mesh.devices.reshape(2, 8, 8, 2, 2), ("xl", "z", "y", "xh", "core"))
    dense = ("xl", "z", "y")
    every = ("xl", "z", "y", "xh", "core")
    in_specs = (
        P(EMB, None),
        P(EMB, None),
        P(dense, None),
        P(every, None, None),
        P(every, None),
        P(every, None),
        P(dense),
        P(every, None),
        P(None, TPA),
        P(TPA, None),
        P(),
        P(),
    )
    out_specs = (
        P(EMB, None),
        P(EMB, None),
        P(every, None),
        P(dense, TPA),
        P(TPA, dense),
        P(dense),
        P(dense),
    )
    return jax.shard_map(local, mesh=fine, in_specs=in_specs, out_specs=out_specs, check_vma=False)
```

```python
import jax
import jax.numpy as jnp
from jax import lax
from jax.experimental import pallas as pl
from jax.experimental.pallas import tpu as pltpu
from jax.sharding import Mesh, PartitionSpec as P

BF = jnp.bfloat16
F32 = jnp.float32
I32 = jnp.int32
E = 128
F = 13
BAG = 4
LOOK = F * BAG
N = 64
DENSE = 256
TP = 4
DP = 8
SHARDS = 16
CAP = 312
ROWS = 1024
DX = 1792
POOL = F * E
RANK = 128
GROUP = 14
CHUNK = 32
XROWS = 80
BLOCKS = DX // E
BAGS = N * F
LEARN = 0.5
EMB = ("xl", "z")
TPA = ("xh", "core")

VMEM = pl.BlockSpec(memory_space=pltpu.VMEM)
SMEM = pl.BlockSpec(memory_space=pltpu.SMEM)


def iota(shape, axis):
    return lax.broadcasted_iota(I32, shape, axis)


def dot(a, b, ca=1, cb=0):
    return lax.dot_general(a, b, (((ca,), (cb,)), ((), ())), preferred_element_type=F32)


def call(kernel, outs, ins, name, scratch=(), limit=40, flops=0):
    nbytes = sum(x.size * x.dtype.itemsize for x in ins)
    return pl.pallas_call(
        kernel,
        out_shape=outs,
        in_specs=[SMEM if x.size < 8 else VMEM for x in ins],
        out_specs=jax.tree.map(lambda _: VMEM, outs),
        scratch_shapes=scratch,
        compiler_params=pltpu.CompilerParams(vmem_limit_bytes=limit << 20),
        cost_estimate=pl.CostEstimate(flops=flops, bytes_accessed=nbytes, transcendentals=0),
        name=name,
    )(*ins)


def index_kernel(
    shard_ref, row_ref, len_ref, down_ref, up_ref, ids_ref, src_ref, src_t_ref, pack_ref
):
    def spread(values):
        parts = []
        for j in range(BAG):
            pick = (iota((F, LOOK), 1) == BAG * iota((F, LOOK), 0) + j).astype(F32).astype(BF)
            parts.append(dot(pick, values.astype(F32).astype(BF)))
        return jnp.concatenate(parts, axis=1)

    for j in range(DX // E):
        pack_ref[j] = down_ref[j * E : (j + 1) * E, :]
        pack_ref[DX // E + j] = up_ref[:, j * E : (j + 1) * E]
    shard = spread(shard_ref[...].reshape(LOOK, N))
    rows = row_ref[...]
    row_lo, row_hi = spread(rows & 255), spread(rows >> 8)
    lens = len_ref[...].astype(F32)
    lens = jnp.concatenate([lens] * BAG, axis=1)
    wide = (F, BAG * N)
    lane = iota(wide, 1)
    usable = (lane >> 6).astype(F32) < lens
    bag = jnp.where(usable, iota(wide, 0) * N + (lane & (N - 1)) + 1, 0)
    bag_lo, bag_hi = (bag & 255).astype(F32), (bag & ~255).astype(F32)
    row_hi = row_hi * 256.0

    sq = (BAG * N, BAG * N)
    upper = (iota(sq, 0) < iota(sq, 1)).astype(F32).astype(BF)
    shards = iota((SHARDS, BAG * N), 0).astype(F32)
    slots = iota((CAP, BAG * N), 0).astype(F32)
    base = jnp.zeros((SHARDS, 1), F32)
    ids = jnp.zeros((SHARDS, CAP), F32)
    src = jnp.zeros((SHARDS, CAP), F32)
    src_t = jnp.zeros((CAP, SHARDS), F32)
    for f in range(F):
        hit = shards == shard[f : f + 1, :]
        one = jnp.where(hit, 1.0, 0.0)
        before = dot(one.astype(BF), upper) + base
        base = base + jnp.sum(one, axis=1, keepdims=True)
        rank = jnp.sum(one * before, axis=0, keepdims=True)
        place = jnp.where(slots == rank, 1.0, 0.0).astype(BF)

        def put(v):
            return jnp.where(hit, v[f : f + 1, :], 0.0).astype(BF)

        lo, hi = put(bag_lo), put(bag_hi)
        ids = ids + dot(put(row_lo), place, 1, 1) + dot(put(row_hi), place, 1, 1)
        src = src + dot(lo, place, 1, 1) + dot(hi, place, 1, 1)
        src_t = src_t + dot(place, lo, 1, 1) + dot(place, hi, 1, 1)
    ids_ref[...] = ids.astype(I32)
    src_ref[...] = src.astype(I32) - 1
    src_t_ref[...] = src_t.astype(I32) - 1


def fetch_kernel(ids_ref, table_ref, out_ref):
    table = table_ref[...].astype(BF)
    cols = jnp.transpose(ids_ref[...].astype(F32))
    lanes = iota((CAP, ROWS), 1).astype(F32)
    for s in range(SHARDS):
        pick = jnp.where(cols[:, s : s + 1] == lanes, 1.0, 0.0).astype(BF)
        out_ref[s] = dot(pick, table).astype(BF)


def pool_kernel(where_ref, rows_ref, src_ref, dense_ref, out_ref, acc_ref):
    first = pl.multiple_of(where_ref[0] * N, N)
    out_ref[0:N, 0:E] = dense_ref[pl.ds(first, N), :]
    out_ref[N:, :] = jnp.zeros((XROWS - N, DX), BF)
    bags = iota((BAGS, CAP), 0)
    for s in range(SHARDS):
        pick = jnp.where(bags == src_ref[s : s + 1, :], 1.0, 0.0).astype(BF)
        term = dot(pick, rows_ref[s])
        if s == 0:
            acc_ref[...] = term
        else:
            acc_ref[...] += term
    for f in range(F):
        out_ref[0:N, (f + 1) * E : (f + 2) * E] = acc_ref[f * N : (f + 1) * N, :].astype(BF)


def dense_kernel(
    where_ref, x_ref, pack_ref, bias_ref, head_ref, label_ref, feedback_ref, src_t_ref,
    carried_ref, send_ref, small_ref, down_ref, up_ref,
):
    first = pl.multiple_of(where_ref[0] * N, N)
    for k in range(TP):
        block = slice(k * RANK, (k + 1) * RANK)
        for j in range(BLOCKS):
            down_ref[j * E : (j + 1) * E, block] = pack_ref[k, j]
            up_ref[block, j * E : (j + 1) * E] = pack_ref[k, BLOCKS + j]
    x = x_ref[0:N, :]
    hidden = dot(x, down_ref[...]).astype(BF)
    up = up_ref[...]
    crossed = dot(hidden, up)
    xf = x.astype(F32)
    bias, head = bias_ref[...], head_ref[...]
    x_next = xf * (crossed + bias) + xf
    logits = jnp.sum(x_next * head, axis=1, keepdims=True)
    grad_logit = jax.nn.sigmoid(logits) - label_ref[pl.ds(first, N), :].astype(F32)
    grad_next = grad_logit * head
    grad_cross = (grad_next * xf).astype(BF)
    grad_hidden = dot(grad_cross, up, 1, 1).astype(BF)
    back = dot(grad_hidden, down_ref[E:, :], 1, 1)
    carried = grad_next[:, E:] * (crossed[:, E:] + bias[:, E:] + 1.0) + back + feedback_ref[...]
    carried_ref[...] = carried
    sent = carried.astype(BF)
    by_bag = jnp.concatenate([sent[:, f * E : (f + 1) * E] for f in range(F)], axis=0)
    bags = iota((CAP, BAGS), 1)
    for s in range(SHARDS):
        pick = jnp.where(src_t_ref[:, s : s + 1] == bags, 1.0, 0.0).astype(BF)
        send_ref[s] = dot(pick, by_bag).astype(BF)
    small_ref[0:N, :] = jnp.broadcast_to(grad_logit, (N, E))
    grad_head = jnp.sum(grad_logit * x_next, axis=0, keepdims=True)
    for j in range(DX // E):
        small_ref[N + j : N + j + 1, :] = grad_head[:, j * E : (j + 1) * E]
    small_ref[N + DX // E :, :] = jnp.zeros((2, E), F32)


def grads_kernel(
    where_ref, x_ref, down_ref, up_ref, head_ref, s0_ref, s1_ref, s2_ref, s3_ref,
    keep_ref, send_ref, logit_ref, down_grad_ref, up_grad_ref, stage_ref,
):
    t, y, u = where_ref[0], where_ref[1], where_ref[2]
    for m, ref in enumerate((s0_ref, s1_ref, s2_ref, s3_ref)):
        logit_ref[pl.ds(pl.multiple_of((t ^ m) * N, N), N), :] = ref[0:N, :]
    x = jnp.concatenate([x_ref[XROWS * k : XROWS * k + N, :] for k in range(TP)], axis=0)
    xf = x.astype(F32)
    hidden = dot(x, down_ref[...]).astype(BF)
    cross = logit_ref[:, 0:1] * head_ref[...] * xf
    grad_bias = jnp.sum(cross, axis=0, keepdims=True)
    grad_cross = cross.astype(BF)
    grad_hidden = dot(grad_cross, up_ref[...], 1, 1).astype(BF)
    down_grad_ref[...] = dot(x, grad_hidden, 0, 0).astype(BF)
    up_grad_ref[...] = dot(grad_cross, hidden, 0, 0).astype(BF)

    tail = slice(N, N + DX // E)
    heads = (s0_ref[tail, :] + s1_ref[tail, :]) + (s2_ref[tail, :] + s3_ref[tail, :])
    grad_head = jnp.concatenate([heads[j : j + 1, :] for j in range(DX // E)], axis=1)
    groups = DX // GROUP
    r = iota((groups, DX), 1) - GROUP * iota((groups, DX), 0)
    own = (r >= 0) & (r < GROUP)
    rows = iota((DX, E), 0)
    rest14 = rows - GROUP * jnp.floor((rows.astype(F32) + 0.5) * (1.0 / GROUP)).astype(I32)
    small = jnp.zeros((groups, E), F32)
    for p, v in enumerate((grad_head, grad_bias)):
        spread = jnp.where(own, v, 0.0).astype(BF)
        lanes = jnp.where(iota((DX, E), 1) == rest14 + 16 * p, 1.0, 0.0).astype(BF)
        small = small + dot(spread, lanes)

    block = DP * GROUP
    q = (DP * CHUNK, 2 * block + 32)
    d, rho, col = iota(q, 0) >> 5, iota(q, 0) & 31, iota(q, 1)
    want = jnp.where(
        rho < GROUP,
        GROUP * d + rho,
        jnp.where(
            rho < 2 * GROUP,
            block + GROUP * d + rho - GROUP,
            jnp.where(rho == 2 * GROUP, 2 * block + d, -1),
        ),
    )
    select = jnp.where(col == want, 1.0, 0.0).astype(BF)
    for e in range(SHARDS):
        part = jnp.concatenate([small[DP * e : DP * e + DP], jnp.zeros((24, E), F32)], axis=0)
        block_rows = jnp.concatenate(
            [
                down_grad_ref[block * e : block * (e + 1), :],
                up_grad_ref[block * e : block * (e + 1), :],
                part.astype(BF),
            ],
            axis=0,
        )
        got = dot(select, block_rows).astype(BF)
        w = u ^ e
        place = ((w >> 3) & 1) * 8 + (w & 1) * 4 + ((w >> 1) & 3)
        for k in range(DP):
            v = y ^ k
            stage_ref[v & 1, v >> 1, place] = got[CHUNK * k : CHUNK * (k + 1)]
    keep_ref[...] = stage_ref[0]
    send_ref[...] = stage_ref[1]


def scatter_kernel(ids_ref, rows_ref, out_ref, acc_ref):
    rows = iota((ROWS, CAP), 0)
    for s in range(SHARDS):
        pick = jnp.where(rows == ids_ref[s : s + 1, :], 1.0, 0.0).astype(BF)
        term = dot(pick, rows_ref[s])
        if s == 0:
            acc_ref[...] = term
        else:
            acc_ref[...] += term
    out_ref[...] = acc_ref[...].astype(BF)


def total(parts):
    parts = [p.astype(F32) for p in parts]
    while len(parts) > 1:
        parts = [a + b for a, b in zip(parts[::2], parts[1::2])]
    return parts[0]


def sds(shape, dtype):
    return jax.ShapeDtypeStruct(shape, dtype)


def local(
    emb_table, row_accum, dense_input, row_shard, local_row, bag_length, labels, feedback,
    cross_down, cross_up, cross_bias, head_weight,
):
    bias, head = cross_bias.reshape(1, DX), head_weight.reshape(1, DX)
    where = jnp.stack([lax.axis_index(TPA), lax.axis_index("y"), lax.axis_index(EMB)]).astype(I32)
    ids, src, src_t, pack = call(
        index_kernel,
        (
            sds((SHARDS, CAP), I32),
            sds((SHARDS, CAP), I32),
            sds((CAP, SHARDS), I32),
            sds((2 * BLOCKS, E, E), BF),
        ),
        (row_shard.transpose(1, 2, 0), local_row.T, bag_length.T, cross_down, cross_up),
        "index",
        flops=400_000_000,
    )
    with jax.named_scope("gather_weights"):
        pack_all = lax.all_gather(pack, TPA, axis=0, tiled=False)
    ids = lax.all_to_all(ids, EMB, split_axis=0, concat_axis=0, tiled=True)
    fetched = call(
        fetch_kernel, sds((SHARDS, CAP, E), BF), (ids, emb_table), "fetch", flops=1_300_000_000
    )
    returned = lax.all_to_all(fetched, EMB, split_axis=0, concat_axis=0, tiled=True)
    x = call(
        pool_kernel,
        sds((XROWS, DX), BF),
        (where, returned, src, dense_input),
        "pool",
        scratch=[pltpu.VMEM((BAGS, E), F32)],
        flops=1_060_000_000,
    )
    x_all = lax.all_gather(x, TPA, axis=0, tiled=True)
    carried, send, small = call(
        dense_kernel,
        (sds((N, POOL), F32), sds((SHARDS, CAP, E), BF), sds((N + 16, E), F32)),
        (where, x, pack_all, bias, head, labels.reshape(DENSE, 1), feedback, src_t),
        "dense",
        scratch=[pltpu.VMEM((DX, TP * RANK), BF), pltpu.VMEM((TP * RANK, DX), BF)],
        flops=1_500_000_000,
    )
    arrived = lax.all_to_all(send, EMB, split_axis=0, concat_axis=0, tiled=True)

    def partner(value, axes, mask):
        size = lax.axis_size(axes)
        return lax.ppermute(value, axes, [(i, i ^ mask) for i in range(size)])

    s1 = partner(small, TPA, 1)
    s2 = partner(small, TPA, 2)
    s3 = partner(small, TPA, 3)
    keep, give = call(
        grads_kernel,
        [sds((DP // 2, SHARDS, CHUNK, E), BF)] * 2,
        (where, x_all, cross_down, cross_up, head, small, s1, s2, s3),
        "grads",
        scratch=[
            pltpu.VMEM((DENSE, E), F32),
            pltpu.VMEM((DX, RANK), BF),
            pltpu.VMEM((DX, RANK), BF),
            pltpu.VMEM((2, DP // 2, SHARDS, CHUNK, E), BF),
        ],
        flops=1_000_000_000,
    )
    got = partner(give, "y", 1)
    part = [keep[m].astype(F32) + got[m].astype(F32) for m in range(DP // 2)]
    part = [part[0]] + [p.astype(BF) for p in part[1:]]
    arrived, *part = lax.optimization_barrier((arrived, *part))
    part = part[:1] + [partner(part[m], "y", 2 * m) for m in range(1, DP // 2)]
    row_grad = call(
        scatter_kernel,
        sds((ROWS, E), BF),
        (ids, arrived),
        "scatter",
        scratch=[pltpu.VMEM((ROWS, E), F32)],
        flops=1_300_000_000,
    )
    owners = ("y", "core")
    pieces = 2 * DP
    by_y = lax.all_to_all(row_grad, owners, split_axis=0, concat_axis=0, tiled=True)
    over_y = total(part)
    part = [over_y[0:4]] + [over_y[4 * c : 4 * c + 4].astype(BF) for c in (1, 2, 3)]
    by_y, *part = lax.optimization_barrier((by_y, *part))
    part = part[:1] + [partner(part[c], EMB, mask) for c, mask in ((1, 1), (2, 8), (3, 9))]
    mine = jnp.sum(by_y.reshape(pieces, ROWS // pieces, E).astype(F32), axis=0)
    mine = (mine + partner(mine, "xh", 1)).astype(BF)
    spread = jnp.broadcast_to(mine[None], (pieces, ROWS // pieces, E)).reshape(ROWS, E)
    full = lax.all_to_all(spread, owners, split_axis=0, concat_axis=0, tiled=True)
    over_pair = total(part)
    part = [over_pair[0]] + [over_pair[i].astype(BF) for i in (1, 2, 3)]
    full, *part = lax.optimization_barrier((full, *part))
    part = part[:1] + [partner(part[i], EMB, 2 * i) for i in (1, 2, 3)]
    full = full.astype(F32)
    accum_new = row_accum + full * full
    table_new = emb_table - LEARN * full / jnp.sqrt(accum_new)
    grads = total(part)
    grad_down = grads[0:GROUP]
    grad_up = grads[GROUP : 2 * GROUP].T
    grad_head = grads[2 * GROUP, 0:GROUP]
    grad_bias = grads[2 * GROUP, 16 : 16 + GROUP]

    return (table_new, accum_new, carried, grad_down, grad_up, grad_bias, grad_head)


def solution(mesh):
    fine = Mesh(mesh.devices.reshape(2, 8, 8, 2, 2), ("xl", "z", "y", "xh", "core"))
    dense = ("xl", "z", "y")
    every = ("xl", "z", "y", "xh", "core")
    in_specs = (
        P(EMB, None),
        P(EMB, None),
        P(dense, None),
        P(every, None, None),
        P(every, None),
        P(every, None),
        P(dense),
        P(every, None),
        P(None, TPA),
        P(TPA, None),
        P(),
        P(),
    )
    out_specs = (
        P(EMB, None),
        P(EMB, None),
        P(every, None),
        P(dense, TPA),
        P(TPA, dense),
        P(dense),
        P(dense),
    )
    return jax.shard_map(local, mesh=fine, in_specs=in_specs, out_specs=out_specs, check_vma=False)
```

```python
import jax
import jax.numpy as jnp
from jax import lax
from jax.experimental import pallas as pl
from jax.experimental.pallas import tpu as pltpu
from jax.sharding import Mesh, PartitionSpec as P

BF = jnp.bfloat16
F32 = jnp.float32
I32 = jnp.int32
E = 128
F = 13
BAG = 4
LOOK = F * BAG
N = 64
DENSE = 256
TP = 4
DP = 8
SHARDS = 16
CAP = 312
ROWS = 1024
DX = 1792
POOL = F * E
RANK = 128
GROUP = 14
CHUNK = 32
EARLY = 4
SPAN = POOL + E
BLOCKS = DX // E
BAGS = N * F
LEARN = 0.5
EMB = ("xl", "z")
TPA = ("xh", "core")

VMEM = pl.BlockSpec(memory_space=pltpu.VMEM)
SMEM = pl.BlockSpec(memory_space=pltpu.SMEM)
ANY = pl.BlockSpec(memory_space=pl.ANY)


def iota(shape, axis):
    return lax.broadcasted_iota(I32, shape, axis)


def dot(a, b, ca=1, cb=0):
    return lax.dot_general(a, b, (((ca,), (cb,)), ((), ())), preferred_element_type=F32)


def call(kernel, outs, ins, name, scratch=(), limit=40, flops=0, far=(), far_out=()):
    nbytes = sum(x.size * x.dtype.itemsize for x in ins)
    return pl.pallas_call(
        kernel,
        out_shape=outs,
        in_specs=[SMEM if x.size < 8 else ANY if i in far else VMEM for i, x in enumerate(ins)],
        out_specs=[ANY if i in far_out else VMEM for i in range(len(outs))],
        scratch_shapes=scratch,
        compiler_params=pltpu.CompilerParams(vmem_limit_bytes=limit << 20),
        cost_estimate=pl.CostEstimate(flops=flops, bytes_accessed=nbytes, transcendentals=0),
        name=name,
    )(*ins)


def index_kernel(
    shard_hbm, row_hbm, len_hbm, down_ref, up_ref, ids_ref, src_ref, src_t_ref, pack_ref,
    shard_ref, row_ref, len_ref, sems,
):
    moves = [(shard_hbm, shard_ref), (row_hbm, row_ref), (len_hbm, len_ref)]
    moves.append((down_ref, pack_ref.at[pl.ds(0, DX), :]))
    for j in range(BLOCKS):
        moves.append((up_ref.at[:, pl.ds(j * E, E)], pack_ref.at[pl.ds(DX + j * E, E), :]))
    moves = [pltpu.make_async_copy(a, b, sems.at[i]) for i, (a, b) in enumerate(moves)]
    for move in moves:
        move.start()
    for move in moves[:3]:
        move.wait()

    def spread(values):
        parts = []
        for j in range(BAG):
            pick = (iota((F, LOOK), 1) == BAG * iota((F, LOOK), 0) + j).astype(F32).astype(BF)
            parts.append(dot(pick, values.astype(F32).astype(BF)))
        return jnp.concatenate(parts, axis=1)

    shard = spread(shard_ref[...].reshape(LOOK, N))
    rows = row_ref[...]
    row_lo, row_hi = spread(rows & 255), spread(rows >> 8)
    lens = len_ref[...].astype(F32)
    lens = jnp.concatenate([lens] * BAG, axis=1)
    wide = (F, BAG * N)
    lane = iota(wide, 1)
    usable = (lane >> 6).astype(F32) < lens
    bag = jnp.where(usable, iota(wide, 0) * N + (lane & (N - 1)) + 1, 0)
    bag_lo, bag_hi = (bag & 255).astype(F32), (bag & ~255).astype(F32)
    row_hi = row_hi * 256.0

    sq = (BAG * N, BAG * N)
    upper = (iota(sq, 0) < iota(sq, 1)).astype(F32).astype(BF)
    shards = iota((SHARDS, BAG * N), 0).astype(F32)
    slots = iota((CAP, BAG * N), 0).astype(F32)
    base = jnp.zeros((SHARDS, 1), F32)
    ids = jnp.zeros((SHARDS, CAP), F32)
    src = jnp.zeros((SHARDS, CAP), F32)
    src_t = jnp.zeros((CAP, SHARDS), F32)
    for f in range(F):
        hit = shards == shard[f : f + 1, :]
        one = jnp.where(hit, 1.0, 0.0)
        before = dot(one.astype(BF), upper) + base
        base = base + jnp.sum(one, axis=1, keepdims=True)
        rank = jnp.sum(one * before, axis=0, keepdims=True)
        place = jnp.where(slots == rank, 1.0, 0.0).astype(BF)

        def put(v):
            return jnp.where(hit, v[f : f + 1, :], 0.0).astype(BF)

        lo, hi = put(bag_lo), put(bag_hi)
        ids = ids + dot(put(row_lo), place, 1, 1) + dot(put(row_hi), place, 1, 1)
        src = src + dot(lo, place, 1, 1) + dot(hi, place, 1, 1)
        src_t = src_t + dot(place, lo, 1, 1) + dot(place, hi, 1, 1)
    ids_ref[...] = ids.astype(I32)
    src_ref[...] = src.astype(I32) - 1
    src_t_ref[...] = src_t.astype(I32) - 1
    for move in moves[3:]:
        move.wait()


def fetch_kernel(ids_ref, table_ref, out_ref):
    table = table_ref[...].astype(BF)
    cols = jnp.transpose(ids_ref[...].astype(F32))
    lanes = iota((CAP, ROWS), 1).astype(F32)
    for s in range(SHARDS):
        pick = jnp.where(cols[:, s : s + 1] == lanes, 1.0, 0.0).astype(BF)
        out_ref[s] = dot(pick, table).astype(BF)


def main_kernel(
    where_ref, rows_ref, src_ref, dense_ref, pack_ref, bias_ref, head_ref, label_ref,
    feedback_ref, src_t_ref, carried_ref, send_ref, span_ref,
    acc_ref, x_ref, down_ref, up_ref, small_ref, sems,
):
    moves = []
    for k in range(TP):
        block = pl.ds(k * RANK, RANK)
        moves.append((pack_ref.at[k, pl.ds(0, DX), :], down_ref.at[:, block]))
        for j in range(BLOCKS):
            lanes = pl.ds(j * E, E)
            moves.append((pack_ref.at[k, pl.ds(DX + j * E, E), :], up_ref.at[block, lanes]))
    moves = [pltpu.make_async_copy(a, b, sems.at[i]) for i, (a, b) in enumerate(moves)]
    for move in moves:
        move.start()

    first = pl.multiple_of(where_ref[0] * N, N)
    x_ref[:, 0:E] = dense_ref[pl.ds(first, N), :]
    bags = iota((BAGS, CAP), 0)
    for s in range(SHARDS):
        pick = jnp.where(bags == src_ref[s : s + 1, :], 1.0, 0.0).astype(BF)
        term = dot(pick, rows_ref[s])
        if s == 0:
            acc_ref[...] = term
        else:
            acc_ref[...] += term
    for f in range(F):
        pooled = acc_ref[f * N : (f + 1) * N, :].astype(BF)
        x_ref[:, (f + 1) * E : (f + 2) * E] = pooled
        span_ref[:, f * E : (f + 1) * E] = pooled
    for move in moves:
        move.wait()
    x = x_ref[...]
    hidden = dot(x, down_ref[...]).astype(BF)
    up = up_ref[...]
    crossed = dot(hidden, up)
    xf = x.astype(F32)
    bias, head = bias_ref[...], head_ref[...]
    x_next = xf * (crossed + bias) + xf
    logits = jnp.sum(x_next * head, axis=1, keepdims=True)
    grad_logit = jax.nn.sigmoid(logits) - label_ref[pl.ds(first, N), :].astype(F32)
    grad_next = grad_logit * head
    grad_cross = (grad_next * xf).astype(BF)
    grad_hidden = dot(grad_cross, up, 1, 1).astype(BF)
    back = dot(grad_hidden, down_ref[E:, :], 1, 1)
    carried = grad_next[:, E:] * (crossed[:, E:] + bias[:, E:] + 1.0) + back + feedback_ref[...]
    carried_ref[...] = carried
    sent = carried.astype(BF)
    by_bag = jnp.concatenate([sent[:, f * E : (f + 1) * E] for f in range(F)], axis=0)
    bags = iota((CAP, BAGS), 1)
    for s in range(SHARDS):
        pick = jnp.where(src_t_ref[:, s : s + 1] == bags, 1.0, 0.0).astype(BF)
        send_ref[s] = dot(pick, by_bag).astype(BF)
    grad_head = jnp.sum(grad_logit * x_next, axis=0, keepdims=True)
    small_ref[...] = jnp.zeros((N, E), F32)
    for j in range(BLOCKS):
        part = grad_head[:, j * E : (j + 1) * E]
        high = part.astype(BF).astype(F32)
        small_ref[j : j + 1, :] = high
        small_ref[BLOCKS + j : BLOCKS + j + 1, :] = part - high
    diagonal = iota((N, N), 0) == iota((N, N), 1)
    part = jnp.sum(jnp.where(diagonal, grad_logit, 0.0), axis=0, keepdims=True)
    high = part.astype(BF).astype(F32)
    small_ref[2 * BLOCKS : 2 * BLOCKS + 1, 0:N] = high
    small_ref[2 * BLOCKS + 1 : 2 * BLOCKS + 2, 0:N] = part - high
    span_ref[:, POOL:] = small_ref[...].astype(BF)


def grads_kernel(where_ref, s0_ref, s1_ref, s2_ref, s3_ref, dense_ref, down_ref, up_ref, head_ref, *rest):
    outs, (x_ref, logit_ref, down_grad_ref, up_grad_ref, stage_ref) = rest[:DP], rest[DP:]
    t, y, u = where_ref[0], where_ref[1], where_ref[2]
    x_ref[:, 0:E] = dense_ref[...]
    diagonal = iota((N, N), 0) == iota((N, N), 1)
    heads = []
    for m, ref in enumerate((s0_ref, s1_ref, s2_ref, s3_ref)):
        rows = pl.ds(pl.multiple_of((t ^ m) * N, N), N)
        x_ref[rows, E:] = ref[:, :POOL]
        tail = ref[:, POOL:].astype(F32)
        heads.append(tail[0:BLOCKS] + tail[BLOCKS : 2 * BLOCKS])
        row = tail[2 * BLOCKS : 2 * BLOCKS + 1, 0:N] + tail[2 * BLOCKS + 1 : 2 * BLOCKS + 2, 0:N]
        logit_ref[rows, :] = jnp.sum(jnp.where(diagonal, row, 0.0), axis=1, keepdims=True)
    heads = (heads[0] + heads[1]) + (heads[2] + heads[3])
    x = x_ref[...]
    grad_logit = logit_ref[...]
    xf = x.astype(F32)
    hidden = dot(x, down_ref[...]).astype(BF)
    cross = grad_logit * head_ref[...] * xf
    grad_bias = jnp.sum(cross, axis=0, keepdims=True)
    grad_cross = cross.astype(BF)
    grad_hidden = dot(grad_cross, up_ref[...], 1, 1).astype(BF)
    down_grad_ref[...] = dot(x, grad_hidden, 0, 0).astype(BF)
    up_grad_ref[...] = dot(grad_cross, hidden, 0, 0).astype(BF)

    grad_head = jnp.concatenate([heads[j : j + 1, :] for j in range(DX // E)], axis=1)
    groups = DX // GROUP
    r = iota((groups, DX), 1) - GROUP * iota((groups, DX), 0)
    own = (r >= 0) & (r < GROUP)
    rows = iota((DX, E), 0)
    rest14 = rows - GROUP * jnp.floor((rows.astype(F32) + 0.5) * (1.0 / GROUP)).astype(I32)
    small = jnp.zeros((groups, E), F32)
    for p, v in enumerate((grad_head, grad_bias)):
        spread = jnp.where(own, v, 0.0).astype(BF)
        lanes = jnp.where(iota((DX, E), 1) == rest14 + 16 * p, 1.0, 0.0).astype(BF)
        small = small + dot(spread, lanes)

    block = DP * GROUP
    q = (DP * CHUNK, 2 * block + 32)
    d, rho, col = iota(q, 0) >> 5, iota(q, 0) & 31, iota(q, 1)
    want = jnp.where(
        rho < GROUP,
        GROUP * d + rho,
        jnp.where(
            rho < 2 * GROUP,
            block + GROUP * d + rho - GROUP,
            jnp.where(rho == 2 * GROUP, 2 * block + d, -1),
        ),
    )
    select = jnp.where(col == want, 1.0, 0.0).astype(BF)
    for e in range(SHARDS):
        part = jnp.concatenate([small[DP * e : DP * e + DP], jnp.zeros((24, E), F32)], axis=0)
        block_rows = jnp.concatenate(
            [
                down_grad_ref[block * e : block * (e + 1), :],
                up_grad_ref[block * e : block * (e + 1), :],
                part.astype(BF),
            ],
            axis=0,
        )
        got = dot(select, block_rows).astype(BF)
        w = u ^ e
        place = ((w >> 3) & 1) * 8 + (w & 1) * 4 + ((w >> 1) & 3)
        for k in range(DP):
            stage_ref[y ^ k, place] = got[CHUNK * k : CHUNK * (k + 1)]
    for m in range(DP):
        outs[m][...] = stage_ref[m]


def scatter_kernel(ids_ref, rows_ref, out_ref, acc_ref):
    rows = iota((ROWS, CAP), 0)
    for s in range(SHARDS):
        pick = jnp.where(rows == ids_ref[s : s + 1, :], 1.0, 0.0).astype(BF)
        term = dot(pick, rows_ref[s])
        if s == 0:
            acc_ref[...] = term
        else:
            acc_ref[...] += term
    out_ref[...] = acc_ref[...].astype(BF)


def total(parts):
    parts = [p.astype(F32) for p in parts]
    while len(parts) > 1:
        parts = [a + b for a, b in zip(parts[::2], parts[1::2])]
    return parts[0]


def sds(shape, dtype):
    return jax.ShapeDtypeStruct(shape, dtype)


def local(
    emb_table, row_accum, dense_input, row_shard, local_row, bag_length, labels, feedback,
    cross_down, cross_up, cross_bias, head_weight,
):
    bias, head = cross_bias.reshape(1, DX), head_weight.reshape(1, DX)
    where = jnp.stack([lax.axis_index(TPA), lax.axis_index("y"), lax.axis_index(EMB)]).astype(I32)
    ids, src, src_t, pack = call(
        index_kernel,
        (
            sds((SHARDS, CAP), I32),
            sds((SHARDS, CAP), I32),
            sds((CAP, SHARDS), I32),
            sds((2 * DX, E), BF),
        ),
        (row_shard.transpose(1, 2, 0), local_row.T, bag_length.T, cross_down, cross_up),
        "index",
        scratch=[
            pltpu.VMEM((LOOK, 1, N), I32),
            pltpu.VMEM((LOOK, N), I32),
            pltpu.VMEM((F, N), I32),
            pltpu.SemaphoreType.DMA((4 + BLOCKS,)),
        ],
        flops=400_000_000,
        limit=56,
        far=range(5),
        far_out=(3,),
    )
    with jax.named_scope("gather_weights"):
        pack_all = lax.all_gather(pack, TPA, axis=0, tiled=False)
    ids = lax.all_to_all(ids, EMB, split_axis=0, concat_axis=0, tiled=True)
    (fetched,) = call(
        fetch_kernel, [sds((SHARDS, CAP, E), BF)], (ids, emb_table), "fetch", flops=1_300_000_000
    )
    returned = lax.all_to_all(fetched, EMB, split_axis=0, concat_axis=0, tiled=True)
    carried, send, span = call(
        main_kernel,
        (sds((N, POOL), F32), sds((SHARDS, CAP, E), BF), sds((N, SPAN), BF)),
        (
            where, returned, src, dense_input, pack_all, bias, head, labels.reshape(DENSE, 1),
            feedback, src_t,
        ),
        "main",
        scratch=[
            pltpu.VMEM((BAGS, E), F32),
            pltpu.VMEM((N, DX), BF),
            pltpu.VMEM((DX, TP * RANK), BF),
            pltpu.VMEM((TP * RANK, DX), BF),
            pltpu.VMEM((N, E), F32),
            pltpu.SemaphoreType.DMA((TP * (1 + BLOCKS),)),
        ],
        flops=2_600_000_000,
        limit=56,
        far=(4,),
    )
    arrived = lax.all_to_all(send, EMB, split_axis=0, concat_axis=0, tiled=True)

    def partner(value, axes, mask):
        size = lax.axis_size(axes)
        return lax.ppermute(value, axes, [(i, i ^ mask) for i in range(size)])

    spans = [span] + [partner(span, TPA, m) for m in range(1, TP)]
    part = call(
        grads_kernel,
        [sds((SHARDS, CHUNK, E), BF)] * DP,
        (where, *spans, dense_input, cross_down, cross_up, head),
        "grads",
        scratch=[
            pltpu.VMEM((DENSE, DX), BF),
            pltpu.VMEM((DENSE, 1), F32),
            pltpu.VMEM((DX, RANK), BF),
            pltpu.VMEM((DX, RANK), BF),
            pltpu.VMEM((DP, SHARDS, CHUNK, E), BF),
        ],
        flops=1_000_000_000,
    )
    early = [partner(part[m], "y", m) for m in range(1, EARLY)]
    arrived, *early = lax.optimization_barrier((arrived, *early))
    (row_grad,) = call(
        scatter_kernel,
        [sds((ROWS, E), BF)],
        (ids, arrived),
        "scatter",
        scratch=[pltpu.VMEM((ROWS, E), F32)],
        flops=1_300_000_000,
    )
    row_grad, *late = lax.optimization_barrier((row_grad, *part[EARLY:]))
    late = [partner(v, "y", m) for m, v in enumerate(late, EARLY)]
    part = [part[0], *early, *late]
    owners = ("y", "core")
    pieces = 2 * DP
    by_y = lax.all_to_all(row_grad, owners, split_axis=0, concat_axis=0, tiled=True)
    over_y = total(part)
    part = [over_y[0:4]] + [over_y[4 * c : 4 * c + 4].astype(BF) for c in (1, 2, 3)]
    by_y, *part = lax.optimization_barrier((by_y, *part))
    part = part[:1] + [partner(part[c], EMB, mask) for c, mask in ((1, 1), (2, 8), (3, 9))]
    mine = jnp.sum(by_y.reshape(pieces, ROWS // pieces, E).astype(F32), axis=0)
    mine = (mine + partner(mine, "xh", 1)).astype(BF)
    spread = jnp.broadcast_to(mine[None], (pieces, ROWS // pieces, E)).reshape(ROWS, E)
    full = lax.all_to_all(spread, owners, split_axis=0, concat_axis=0, tiled=True)
    over_pair = total(part)
    part = [over_pair[0]] + [over_pair[i].astype(BF) for i in (1, 2, 3)]
    full, *part = lax.optimization_barrier((full, *part))
    part = part[:1] + [partner(part[i], EMB, 2 * i) for i in (1, 2, 3)]
    full = full.astype(F32)
    accum_new = row_accum + full * full
    table_new = emb_table - LEARN * full / jnp.sqrt(accum_new)
    grads = total(part)
    grad_down = grads[0:GROUP]
    grad_up = grads[GROUP : 2 * GROUP].T
    grad_head = grads[2 * GROUP, 0:GROUP]
    grad_bias = grads[2 * GROUP, 16 : 16 + GROUP]

    return (table_new, accum_new, carried, grad_down, grad_up, grad_bias, grad_head)


def solution(mesh):
    fine = Mesh(mesh.devices.reshape(2, 8, 8, 2, 2), ("xl", "z", "y", "xh", "core"))
    dense = ("xl", "z", "y")
    every = ("xl", "z", "y", "xh", "core")
    in_specs = (
        P(EMB, None),
        P(EMB, None),
        P(dense, None),
        P(every, None, None),
        P(every, None),
        P(every, None),
        P(dense),
        P(every, None),
        P(None, TPA),
        P(TPA, None),
        P(),
        P(),
    )
    out_specs = (
        P(EMB, None),
        P(EMB, None),
        P(every, None),
        P(dense, TPA),
        P(TPA, dense),
        P(dense),
        P(dense),
    )
    return jax.shard_map(local, mesh=fine, in_specs=in_specs, out_specs=out_specs, check_vma=False)
```

```python
import jax
import jax.numpy as jnp
from jax import lax
from jax.experimental import pallas as pl
from jax.experimental.pallas import tpu as pltpu
from jax.sharding import Mesh, PartitionSpec as P

BF = jnp.bfloat16
F32 = jnp.float32
I32 = jnp.int32
E = 128
F = 13
BAG = 4
LOOK = F * BAG
N = 64
DENSE = 256
TP = 4
DP = 8
SHARDS = 16
CAP = 312
ROWS = 1024
DX = 1792
POOL = F * E
RANK = 128
GROUP = 14
CHUNK = 32
BLOCKS = DX // E
BAGS = N * F
LEARN = 0.5
EMB = ("xl", "z")
TPA = ("xh", "core")

VMEM = pl.BlockSpec(memory_space=pltpu.VMEM)
SMEM = pl.BlockSpec(memory_space=pltpu.SMEM)
ANY = pl.BlockSpec(memory_space=pl.ANY)


def iota(shape, axis):
    return lax.broadcasted_iota(I32, shape, axis)


def dot(a, b, ca=1, cb=0):
    return lax.dot_general(a, b, (((ca,), (cb,)), ((), ())), preferred_element_type=F32)


def call(kernel, outs, ins, name, scratch=(), limit=40, flops=0, far=()):
    nbytes = sum(x.size * x.dtype.itemsize for x in ins)
    return pl.pallas_call(
        kernel,
        out_shape=outs,
        in_specs=[SMEM if x.size < 8 else ANY if i in far else VMEM for i, x in enumerate(ins)],
        out_specs=[VMEM] * len(outs),
        scratch_shapes=scratch,
        compiler_params=pltpu.CompilerParams(vmem_limit_bytes=limit << 20),
        cost_estimate=pl.CostEstimate(flops=flops, bytes_accessed=nbytes, transcendentals=0),
        name=name,
    )(*ins)


def index_kernel(
    shard_hbm, row_hbm, len_hbm, down_hbm, up_hbm, ids_ref, src_ref, src_t_ref, pack_ref,
    shard_ref, row_ref, len_ref, up_ref, sems,
):
    moves = [(shard_hbm, shard_ref), (row_hbm, row_ref), (len_hbm, len_ref)]
    moves += [(down_hbm, pack_ref.at[pl.ds(0, DX), :]), (up_hbm, up_ref)]
    moves = [pltpu.make_async_copy(a, b, sems.at[i]) for i, (a, b) in enumerate(moves)]
    for move in moves:
        move.start()
    for move in moves[:3]:
        move.wait()

    def spread(values):
        parts = []
        for j in range(BAG):
            pick = (iota((F, LOOK), 1) == BAG * iota((F, LOOK), 0) + j).astype(F32).astype(BF)
            parts.append(dot(pick, values.astype(F32).astype(BF)))
        return jnp.concatenate(parts, axis=1)

    shard = spread(shard_ref[...].reshape(LOOK, N))
    rows = row_ref[...]
    row_lo, row_hi = spread(rows & 255), spread(rows >> 8)
    lens = len_ref[...].astype(F32)
    lens = jnp.concatenate([lens] * BAG, axis=1)
    wide = (F, BAG * N)
    lane = iota(wide, 1)
    usable = (lane >> 6).astype(F32) < lens
    bag = jnp.where(usable, iota(wide, 0) * N + (lane & (N - 1)) + 1, 0)
    bag_lo, bag_hi = (bag & 255).astype(F32), (bag & ~255).astype(F32)
    row_hi = row_hi * 256.0

    sq = (BAG * N, BAG * N)
    upper = (iota(sq, 0) < iota(sq, 1)).astype(F32).astype(BF)
    shards = iota((SHARDS, BAG * N), 0).astype(F32)
    slots = iota((CAP, BAG * N), 0).astype(F32)
    base = jnp.zeros((SHARDS, 1), F32)
    ids = jnp.zeros((SHARDS, CAP), F32)
    src = jnp.zeros((SHARDS, CAP), F32)
    src_t = jnp.zeros((CAP, SHARDS), F32)
    for f in range(F):
        hit = shards == shard[f : f + 1, :]
        one = jnp.where(hit, 1.0, 0.0)
        before = dot(one.astype(BF), upper) + base
        base = base + jnp.sum(one, axis=1, keepdims=True)
        rank = jnp.sum(one * before, axis=0, keepdims=True)
        place = jnp.where(slots == rank, 1.0, 0.0).astype(BF)

        def put(v):
            return jnp.where(hit, v[f : f + 1, :], 0.0).astype(BF)

        lo, hi = put(bag_lo), put(bag_hi)
        ids = ids + dot(put(row_lo), place, 1, 1) + dot(put(row_hi), place, 1, 1)
        src = src + dot(lo, place, 1, 1) + dot(hi, place, 1, 1)
        src_t = src_t + dot(place, lo, 1, 1) + dot(place, hi, 1, 1)
    ids_ref[...] = ids.astype(I32)
    src_ref[...] = src.astype(I32) - 1
    src_t_ref[...] = src_t.astype(I32) - 1
    for move in moves[3:]:
        move.wait()
    for j in range(BLOCKS):
        pack_ref[DX + j * E : DX + (j + 1) * E, :] = up_ref[:, j * E : (j + 1) * E]


def fetch_kernel(ids_ref, table_ref, out_ref):
    table = table_ref[...].astype(BF)
    cols = jnp.transpose(ids_ref[...].astype(F32))
    lanes = iota((CAP, ROWS), 1).astype(F32)
    for s in range(SHARDS):
        pick = jnp.where(cols[:, s : s + 1] == lanes, 1.0, 0.0).astype(BF)
        out_ref[s] = dot(pick, table).astype(BF)


def start_weights(pack_ref, down_ref, up_ref, sems):
    moves = []
    for k in range(TP):
        block = pl.ds(k * RANK, RANK)
        moves.append((pack_ref.at[k, pl.ds(0, DX), :], down_ref.at[:, block]))
        for j in range(BLOCKS):
            lanes = pl.ds(j * E, E)
            moves.append((pack_ref.at[k, pl.ds(DX + j * E, E), :], up_ref.at[block, lanes]))
    moves = [pltpu.make_async_copy(a, b, sems.at[i]) for i, (a, b) in enumerate(moves)]
    for move in moves:
        move.start()
    return moves


def forward(x, down, up, bias, head, labels):
    hidden = dot(x, down).astype(BF)
    crossed = dot(hidden, up)
    xf = x.astype(F32)
    x_next = xf * (crossed + bias) + xf
    logits = jnp.sum(x_next * head, axis=1, keepdims=True)
    grad_logit = jax.nn.sigmoid(logits) - labels.astype(F32)
    grad_next = grad_logit * head
    return hidden, crossed, xf, x_next, grad_logit, grad_next, grad_next * xf


def pool_kernel(rows_ref, src_ref, pooled_ref, acc_ref):
    bags = iota((BAGS, CAP), 0)
    for s in range(SHARDS):
        pick = jnp.where(bags == src_ref[s : s + 1, :], 1.0, 0.0).astype(BF)
        term = dot(pick, rows_ref[s])
        if s == 0:
            acc_ref[...] = term
        else:
            acc_ref[...] += term
    for f in range(F):
        pooled_ref[:, f * E : (f + 1) * E] = acc_ref[f * N : (f + 1) * N, :].astype(BF)


def main_kernel(
    where_ref, pooled_ref, dense_ref, pack_ref, bias_ref, head_ref, label_ref, feedback_ref,
    src_t_ref, carried_ref, send_ref, down_ref, up_ref, sems,
):
    moves = start_weights(pack_ref, down_ref, up_ref, sems)
    first = pl.multiple_of(where_ref[0] * N, N)
    x = jnp.concatenate([dense_ref[pl.ds(first, N), :], pooled_ref[...]], axis=1)
    for move in moves:
        move.wait()
    up, bias, head = up_ref[...], bias_ref[...], head_ref[...]
    _, crossed, _, _, _, grad_next, cross = forward(
        x, down_ref[...], up, bias, head, label_ref[pl.ds(first, N), :]
    )
    grad_cross = cross.astype(BF)
    grad_hidden = dot(grad_cross, up, 1, 1).astype(BF)
    back = dot(grad_hidden, down_ref[E:, :], 1, 1)
    carried = grad_next[:, E:] * (crossed[:, E:] + bias[:, E:] + 1.0) + back + feedback_ref[...]
    carried_ref[...] = carried
    sent = carried.astype(BF)
    by_bag = jnp.concatenate([sent[:, f * E : (f + 1) * E] for f in range(F)], axis=0)
    bags = iota((CAP, BAGS), 1)
    for s in range(SHARDS):
        pick = jnp.where(src_t_ref[:, s : s + 1] == bags, 1.0, 0.0).astype(BF)
        send_ref[s] = dot(pick, by_bag).astype(BF)


def grads_kernel(
    where_ref, s0_ref, s1_ref, s2_ref, s3_ref, dense_ref, pack_ref, bias_ref, head_ref, label_ref,
    out_ref, x_ref, down_ref, up_ref, hidden_ref, down_grad_ref, up_grad_ref, sems,
):
    moves = start_weights(pack_ref, down_ref, up_ref, sems)
    t = where_ref[0]
    x_ref[:, 0:E] = dense_ref[...]
    for m, ref in enumerate((s0_ref, s1_ref, s2_ref, s3_ref)):
        x_ref[pl.ds(pl.multiple_of((t ^ m) * N, N), N), E:] = ref[...]
    x = x_ref[...]
    for move in moves:
        move.wait()
    hidden, _, _, x_next, grad_logit, _, cross = forward(
        x, down_ref[...], up_ref[...], bias_ref[...], head_ref[...], label_ref[...]
    )
    for k in range(TP):
        hidden_ref[k] = hidden[:, k * RANK : (k + 1) * RANK]
    hidden = hidden_ref[t]
    up = up_ref[pl.ds(pl.multiple_of(t * RANK, RANK), RANK), :]
    grad_cross = cross.astype(BF)
    grad_bias = jnp.sum(cross, axis=0, keepdims=True)
    grad_head = jnp.sum(grad_logit * x_next, axis=0, keepdims=True)
    grad_hidden = dot(grad_cross, up, 1, 1).astype(BF)
    down_grad_ref[...] = dot(x, grad_hidden, 0, 0).astype(BF)
    up_grad_ref[...] = dot(grad_cross, hidden, 0, 0).astype(BF)

    groups = DX // GROUP
    r = iota((groups, DX), 1) - GROUP * iota((groups, DX), 0)
    own = (r >= 0) & (r < GROUP)
    rows = iota((DX, E), 0)
    rest14 = rows - GROUP * jnp.floor((rows.astype(F32) + 0.5) * (1.0 / GROUP)).astype(I32)
    small = jnp.zeros((groups, E), F32)
    for p, v in enumerate((grad_head, grad_bias)):
        spread = jnp.where(own, v, 0.0).astype(BF)
        lanes = jnp.where(iota((DX, E), 1) == rest14 + 16 * p, 1.0, 0.0).astype(BF)
        small = small + dot(spread, lanes)

    block = DP * GROUP
    q = (DP * CHUNK, 2 * block + 32)
    d, rho, col = iota(q, 0) >> 5, iota(q, 0) & 31, iota(q, 1)
    want = jnp.where(
        rho < GROUP,
        GROUP * d + rho,
        jnp.where(
            rho < 2 * GROUP,
            block + GROUP * d + rho - GROUP,
            jnp.where(rho == 2 * GROUP, 2 * block + d, -1),
        ),
    )
    select = jnp.where(col == want, 1.0, 0.0).astype(BF)
    for e in range(SHARDS):
        part = jnp.concatenate([small[DP * e : DP * e + DP], jnp.zeros((24, E), F32)], axis=0)
        block_rows = jnp.concatenate(
            [
                down_grad_ref[block * e : block * (e + 1), :],
                up_grad_ref[block * e : block * (e + 1), :],
                part.astype(BF),
            ],
            axis=0,
        )
        got = dot(select, block_rows).astype(BF)
        for k in range(DP):
            out_ref[k, e] = got[CHUNK * k : CHUNK * (k + 1)]


def scatter_kernel(ids_ref, rows_ref, out_ref, acc_ref):
    rows = iota((ROWS, CAP), 0)
    for s in range(SHARDS):
        pick = jnp.where(rows == ids_ref[s : s + 1, :], 1.0, 0.0).astype(BF)
        term = dot(pick, rows_ref[s])
        if s == 0:
            acc_ref[...] = term
        else:
            acc_ref[...] += term
    out_ref[...] = acc_ref[...].astype(BF)


def partner(value, axes, mask):
    size = lax.axis_size(axes)
    return lax.ppermute(value, axes, [(i, i ^ mask) for i in range(size)])


def sds(shape, dtype):
    return jax.ShapeDtypeStruct(shape, dtype)


def local(
    emb_table, row_accum, dense_input, row_shard, local_row, bag_length, labels, feedback,
    cross_down, cross_up, cross_bias, head_weight,
):
    bias, head = cross_bias.reshape(1, DX), head_weight.reshape(1, DX)
    label = labels.reshape(DENSE, 1)
    where = jnp.stack([lax.axis_index(TPA), lax.axis_index("y"), lax.axis_index(EMB)]).astype(I32)
    ids, src, src_t, pack = call(
        index_kernel,
        (
            sds((SHARDS, CAP), I32),
            sds((SHARDS, CAP), I32),
            sds((CAP, SHARDS), I32),
            sds((2 * DX, E), BF),
        ),
        (row_shard.transpose(1, 2, 0), local_row.T, bag_length.T, cross_down, cross_up),
        "index",
        scratch=[
            pltpu.VMEM((LOOK, 1, N), I32),
            pltpu.VMEM((LOOK, N), I32),
            pltpu.VMEM((F, N), I32),
            pltpu.VMEM((RANK, DX), BF),
            pltpu.SemaphoreType.DMA((5,)),
        ],
        flops=400_000_000,
        limit=56,
        far=range(5),
    )
    with jax.named_scope("gather_weights"):
        pack_all = lax.all_gather(pack, TPA, axis=0, tiled=False)
    ids = lax.all_to_all(ids, EMB, split_axis=0, concat_axis=0, tiled=True)
    (fetched,) = call(
        fetch_kernel, [sds((SHARDS, CAP, E), BF)], (ids, emb_table), "fetch", flops=1_300_000_000
    )
    returned = lax.all_to_all(fetched, EMB, split_axis=0, concat_axis=0, tiled=True)
    (pooled,) = call(
        pool_kernel,
        [sds((N, POOL), BF)],
        (returned, src),
        "pool",
        scratch=[pltpu.VMEM((BAGS, E), F32)],
        flops=1_060_000_000,
    )
    far = partner(pooled, "xh", 1)
    carried, send = call(
        main_kernel,
        (sds((N, POOL), F32), sds((SHARDS, CAP, E), BF)),
        (where, pooled, dense_input, pack_all, bias, head, label, feedback, src_t),
        "main",
        scratch=[
            pltpu.VMEM((DX, TP * RANK), BF),
            pltpu.VMEM((TP * RANK, DX), BF),
            pltpu.SemaphoreType.DMA((TP * (1 + BLOCKS),)),
        ],
        flops=10_000_000_000,
        limit=56,
        far=(3,),
    )
    far, again, send = lax.optimization_barrier((far, pooled, send))
    arrived = lax.all_to_all(send, EMB, split_axis=0, concat_axis=0, tiled=True)

    near, far_near = partner(again, "core", 1), partner(far, "core", 1)
    (part,) = call(
        grads_kernel,
        [sds((DP, SHARDS, CHUNK, E), BF)],
        (where, pooled, near, far, far_near, dense_input, pack_all, bias, head, label),
        "grads",
        scratch=[
            pltpu.VMEM((DENSE, DX), BF),
            pltpu.VMEM((DX, TP * RANK), BF),
            pltpu.VMEM((TP * RANK, DX), BF),
            pltpu.VMEM((TP, DENSE, RANK), BF),
            pltpu.VMEM((DX, RANK), BF),
            pltpu.VMEM((DX, RANK), BF),
            pltpu.SemaphoreType.DMA((TP * (1 + BLOCKS),)),
        ],
        flops=2_000_000_000,
        limit=56,
        far=(6,),
    )
    arrived, part = lax.optimization_barrier((arrived, part))
    over_y = lax.psum_scatter(
        part.reshape(DP * SHARDS * CHUNK, E), "y", scatter_dimension=0, tiled=True
    )
    (row_grad,) = call(
        scatter_kernel,
        [sds((ROWS, E), BF)],
        (ids, arrived),
        "scatter",
        scratch=[pltpu.VMEM((ROWS, E), F32)],
        flops=1_300_000_000,
    )
    owners = ("y", "core")
    pieces = 2 * DP
    by_y = lax.all_to_all(row_grad, owners, split_axis=0, concat_axis=0, tiled=True)
    mine = jnp.sum(by_y.reshape(pieces, ROWS // pieces, E).astype(F32), axis=0)
    mine = (mine + partner(mine, "xh", 1)).astype(BF)
    over_y = over_y.reshape(SHARDS, CHUNK, E)
    over_all = lax.all_to_all(over_y, EMB, split_axis=0, concat_axis=0, tiled=True)
    spread = jnp.broadcast_to(mine[None], (pieces, ROWS // pieces, E)).reshape(ROWS, E)
    spread, over_all = lax.optimization_barrier((spread, over_all))
    full = lax.all_to_all(spread, owners, split_axis=0, concat_axis=0, tiled=True)
    full = full.astype(F32)
    accum_new = row_accum + full * full
    table_new = emb_table - LEARN * full / jnp.sqrt(accum_new)
    grads = jnp.sum(over_all.astype(F32), axis=0)
    grad_down = grads[0:GROUP]
    grad_up = grads[GROUP : 2 * GROUP].T
    grad_head = grads[2 * GROUP, 0:GROUP]
    grad_bias = grads[2 * GROUP, 16 : 16 + GROUP]

    return (table_new, accum_new, carried, grad_down, grad_up, grad_bias, grad_head)


def solution(mesh):
    fine = Mesh(mesh.devices.reshape(2, 8, 8, 2, 2), ("xl", "z", "y", "xh", "core"))
    dense = ("xl", "z", "y")
    every = ("xl", "z", "y", "xh", "core")
    in_specs = (
        P(EMB, None),
        P(EMB, None),
        P(dense, None),
        P(every, None, None),
        P(every, None),
        P(every, None),
        P(dense),
        P(every, None),
        P(None, TPA),
        P(TPA, None),
        P(),
        P(),
    )
    out_specs = (
        P(EMB, None),
        P(EMB, None),
        P(every, None),
        P(dense, TPA),
        P(TPA, dense),
        P(dense),
        P(dense),
    )
    return jax.shard_map(local, mesh=fine, in_specs=in_specs, out_specs=out_specs, check_vma=False)
```

```python
import jax
import jax.numpy as jnp
from jax import lax
from jax.experimental import pallas as pl
from jax.experimental.pallas import tpu as pltpu
from jax.sharding import Mesh, PartitionSpec as P

BF = jnp.bfloat16
F32 = jnp.float32
I32 = jnp.int32
E = 128
F = 13
BAG = 4
LOOK = F * BAG
N = 64
DENSE = 256
TP = 4
DP = 8
SHARDS = 16
CAP = 312
ROWS = 1024
DX = 1792
POOL = F * E
RANK = 128
GROUP = 14
CHUNK = 32
BLOCKS = DX // E
BAGS = N * F
LEARN = 0.5
EMB = ("xl", "z")
TPA = ("xh", "core")

VMEM = pl.BlockSpec(memory_space=pltpu.VMEM)
SMEM = pl.BlockSpec(memory_space=pltpu.SMEM)
ANY = pl.BlockSpec(memory_space=pl.ANY)


def iota(shape, axis):
    return lax.broadcasted_iota(I32, shape, axis)


def dot(a, b, ca=1, cb=0):
    return lax.dot_general(a, b, (((ca,), (cb,)), ((), ())), preferred_element_type=F32)


def call(kernel, outs, ins, name, scratch=(), limit=40, flops=0, far=()):
    nbytes = sum(x.size * x.dtype.itemsize for x in ins)
    return pl.pallas_call(
        kernel,
        out_shape=outs,
        in_specs=[SMEM if x.size < 8 else ANY if i in far else VMEM for i, x in enumerate(ins)],
        out_specs=[VMEM] * len(outs),
        scratch_shapes=scratch,
        compiler_params=pltpu.CompilerParams(vmem_limit_bytes=limit << 20),
        cost_estimate=pl.CostEstimate(flops=flops, bytes_accessed=nbytes, transcendentals=0),
        name=name,
    )(*ins)


def index_kernel(
    shard_hbm, row_hbm, len_hbm, down_hbm, up_hbm, ids_ref, src_ref, src_t_ref, pack_ref,
    shard_ref, row_ref, len_ref, up_ref, sems,
):
    moves = [(shard_hbm, shard_ref), (row_hbm, row_ref), (len_hbm, len_ref)]
    moves += [(down_hbm, pack_ref.at[pl.ds(0, DX), :]), (up_hbm, up_ref)]
    moves = [pltpu.make_async_copy(a, b, sems.at[i]) for i, (a, b) in enumerate(moves)]
    for move in moves:
        move.start()
    for move in moves[:3]:
        move.wait()

    def spread(values):
        parts = []
        for j in range(BAG):
            pick = (iota((F, LOOK), 1) == BAG * iota((F, LOOK), 0) + j).astype(F32).astype(BF)
            parts.append(dot(pick, values.astype(F32).astype(BF)))
        return jnp.concatenate(parts, axis=1)

    shard = spread(shard_ref[...].reshape(LOOK, N))
    rows = row_ref[...]
    row_lo, row_hi = spread(rows & 255), spread(rows >> 8)
    lens = len_ref[...].astype(F32)
    lens = jnp.concatenate([lens] * BAG, axis=1)
    wide = (F, BAG * N)
    lane = iota(wide, 1)
    usable = (lane >> 6).astype(F32) < lens
    bag = jnp.where(usable, iota(wide, 0) * N + (lane & (N - 1)) + 1, 0)
    bag_lo, bag_hi = (bag & 255).astype(F32), (bag & ~255).astype(F32)
    row_hi = row_hi * 256.0

    sq = (BAG * N, BAG * N)
    upper = (iota(sq, 0) < iota(sq, 1)).astype(F32).astype(BF)
    shards = iota((SHARDS, BAG * N), 0).astype(F32)
    slots = iota((CAP, BAG * N), 0).astype(F32)
    base = jnp.zeros((SHARDS, 1), F32)
    found = jnp.zeros((4 * SHARDS, CAP), F32)
    for f in range(F):
        hit = shards == shard[f : f + 1, :]
        one = jnp.where(hit, 1.0, 0.0)
        before = dot(one.astype(BF), upper) + base
        base = base + jnp.sum(one, axis=1, keepdims=True)
        rank = jnp.sum(one * before, axis=0, keepdims=True)
        place = jnp.where(slots == rank, 1.0, 0.0).astype(BF)
        values = [
            jnp.where(hit, v[f : f + 1, :], 0.0) for v in (row_lo, row_hi, bag_lo, bag_hi)
        ]
        found = found + dot(jnp.concatenate(values, axis=0).astype(BF), place, 1, 1)
    ids = found[0:SHARDS] + found[SHARDS : 2 * SHARDS]
    src = found[2 * SHARDS : 3 * SHARDS] + found[3 * SHARDS :] - 1.0
    ids_ref[...] = ids.astype(I32)
    src_ref[...] = src.astype(I32)
    src_t_ref[...] = jnp.transpose(src).astype(I32)
    for move in moves[3:]:
        move.wait()
    for j in range(BLOCKS):
        pack_ref[DX + j * E : DX + (j + 1) * E, :] = up_ref[:, j * E : (j + 1) * E]


def fetch_kernel(ids_ref, table_ref, out_ref):
    table = table_ref[...].astype(BF)
    cols = jnp.transpose(ids_ref[...].astype(F32))
    lanes = iota((CAP, ROWS), 1).astype(F32)
    for s in range(SHARDS):
        pick = jnp.where(cols[:, s : s + 1] == lanes, 1.0, 0.0).astype(BF)
        out_ref[s] = dot(pick, table).astype(BF)


def start_weights(pack_ref, down_ref, up_ref, sems):
    moves = []
    for k in range(TP):
        block = pl.ds(k * RANK, RANK)
        moves.append((pack_ref.at[k, pl.ds(0, DX), :], down_ref.at[:, block]))
        for j in range(BLOCKS):
            lanes = pl.ds(j * E, E)
            moves.append((pack_ref.at[k, pl.ds(DX + j * E, E), :], up_ref.at[block, lanes]))
    moves = [pltpu.make_async_copy(a, b, sems.at[i]) for i, (a, b) in enumerate(moves)]
    for move in moves:
        move.start()
    return moves


def forward(x, down, up, bias, head, labels):
    hidden = dot(x, down).astype(BF)
    crossed = dot(hidden, up)
    xf = x.astype(F32)
    x_next = xf * (crossed + bias) + xf
    logits = jnp.sum(x_next * head, axis=1, keepdims=True)
    grad_logit = jax.nn.sigmoid(logits) - labels.astype(F32)
    grad_next = grad_logit * head
    return hidden, crossed, xf, x_next, grad_logit, grad_next, grad_next * xf


def pool_kernel(rows_ref, src_ref, pooled_ref, acc_ref):
    bags = iota((BAGS, CAP), 0)
    for s in range(SHARDS):
        pick = jnp.where(bags == src_ref[s : s + 1, :], 1.0, 0.0).astype(BF)
        term = dot(pick, rows_ref[s])
        if s == 0:
            acc_ref[...] = term
        else:
            acc_ref[...] += term
    for f in range(F):
        pooled_ref[:, f * E : (f + 1) * E] = acc_ref[f * N : (f + 1) * N, :].astype(BF)


def main_kernel(
    where_ref, pooled_ref, dense_ref, pack_ref, bias_ref, head_ref, label_ref, feedback_ref,
    src_t_ref, carried_ref, send_ref, down_ref, up_ref, sems,
):
    moves = start_weights(pack_ref, down_ref, up_ref, sems)
    first = pl.multiple_of(where_ref[0] * N, N)
    x = jnp.concatenate([dense_ref[pl.ds(first, N), :], pooled_ref[...]], axis=1)
    for move in moves:
        move.wait()
    up, bias, head = up_ref[...], bias_ref[...], head_ref[...]
    _, crossed, _, _, _, grad_next, cross = forward(
        x, down_ref[...], up, bias, head, label_ref[pl.ds(first, N), :]
    )
    grad_cross = cross.astype(BF)
    grad_hidden = dot(grad_cross, up, 1, 1).astype(BF)
    back = dot(grad_hidden, down_ref[E:, :], 1, 1)
    carried = grad_next[:, E:] * (crossed[:, E:] + bias[:, E:] + 1.0) + back + feedback_ref[...]
    carried_ref[...] = carried
    sent = carried.astype(BF)
    by_bag = jnp.concatenate([sent[:, f * E : (f + 1) * E] for f in range(F)], axis=0)
    bags = iota((CAP, BAGS), 1)
    for s in range(SHARDS):
        pick = jnp.where(src_t_ref[:, s : s + 1] == bags, 1.0, 0.0).astype(BF)
        send_ref[s] = dot(pick, by_bag).astype(BF)


def grads_kernel(
    where_ref, s0_ref, s1_ref, s2_ref, s3_ref, dense_ref, pack_ref, bias_ref, head_ref, label_ref,
    out_ref, x_ref, down_ref, up_ref, hidden_ref, down_grad_ref, up_grad_ref, sems,
):
    moves = start_weights(pack_ref, down_ref, up_ref, sems)
    t = where_ref[0]
    x_ref[:, 0:E] = dense_ref[...]
    for m, ref in enumerate((s0_ref, s1_ref, s2_ref, s3_ref)):
        x_ref[pl.ds(pl.multiple_of((t ^ m) * N, N), N), E:] = ref[...]
    x = x_ref[...]
    for move in moves:
        move.wait()
    hidden, _, _, x_next, grad_logit, _, cross = forward(
        x, down_ref[...], up_ref[...], bias_ref[...], head_ref[...], label_ref[...]
    )
    for k in range(TP):
        hidden_ref[k] = hidden[:, k * RANK : (k + 1) * RANK]
    hidden = hidden_ref[t]
    up = up_ref[pl.ds(pl.multiple_of(t * RANK, RANK), RANK), :]
    grad_cross = cross.astype(BF)
    grad_bias = jnp.sum(cross, axis=0, keepdims=True)
    grad_head = jnp.sum(grad_logit * x_next, axis=0, keepdims=True)
    grad_hidden = dot(grad_cross, up, 1, 1).astype(BF)
    down_grad_ref[...] = dot(x, grad_hidden, 0, 0).astype(BF)
    up_grad_ref[...] = dot(grad_cross, hidden, 0, 0).astype(BF)

    groups = DX // GROUP
    r = iota((groups, DX), 1) - GROUP * iota((groups, DX), 0)
    own = (r >= 0) & (r < GROUP)
    rows = iota((DX, E), 0)
    rest14 = rows - GROUP * jnp.floor((rows.astype(F32) + 0.5) * (1.0 / GROUP)).astype(I32)
    small = jnp.zeros((groups, E), F32)
    for p, v in enumerate((grad_head, grad_bias)):
        spread = jnp.where(own, v, 0.0).astype(BF)
        lanes = jnp.where(iota((DX, E), 1) == rest14 + 16 * p, 1.0, 0.0).astype(BF)
        small = small + dot(spread, lanes)

    block = DP * GROUP
    q = (DP * CHUNK, 2 * block + 32)
    d, rho, col = iota(q, 0) >> 5, iota(q, 0) & 31, iota(q, 1)
    want = jnp.where(
        rho < GROUP,
        GROUP * d + rho,
        jnp.where(
            rho < 2 * GROUP,
            block + GROUP * d + rho - GROUP,
            jnp.where(rho == 2 * GROUP, 2 * block + d, -1),
        ),
    )
    select = jnp.where(col == want, 1.0, 0.0).astype(BF)
    for e in range(SHARDS):
        part = jnp.concatenate([small[DP * e : DP * e + DP], jnp.zeros((24, E), F32)], axis=0)
        block_rows = jnp.concatenate(
            [
                down_grad_ref[block * e : block * (e + 1), :],
                up_grad_ref[block * e : block * (e + 1), :],
                part.astype(BF),
            ],
            axis=0,
        )
        got = dot(select, block_rows).astype(BF)
        for k in range(DP):
            out_ref[k, e] = got[CHUNK * k : CHUNK * (k + 1)]


def scatter_kernel(ids_ref, rows_ref, out_ref, acc_ref):
    rows = iota((ROWS, CAP), 0)
    for s in range(SHARDS):
        pick = jnp.where(rows == ids_ref[s : s + 1, :], 1.0, 0.0).astype(BF)
        term = dot(pick, rows_ref[s])
        if s == 0:
            acc_ref[...] = term
        else:
            acc_ref[...] += term
    out_ref[...] = acc_ref[...].astype(BF)


def partner(value, axes, mask):
    size = lax.axis_size(axes)
    return lax.ppermute(value, axes, [(i, i ^ mask) for i in range(size)])


def sds(shape, dtype):
    return jax.ShapeDtypeStruct(shape, dtype)


def local(
    emb_table, row_accum, dense_input, row_shard, local_row, bag_length, labels, feedback,
    cross_down, cross_up, cross_bias, head_weight,
):
    bias, head = cross_bias.reshape(1, DX), head_weight.reshape(1, DX)
    label = labels.reshape(DENSE, 1)
    where = jnp.stack([lax.axis_index(TPA), lax.axis_index("y"), lax.axis_index(EMB)]).astype(I32)
    ids, src, src_t, pack = call(
        index_kernel,
        (
            sds((SHARDS, CAP), I32),
            sds((SHARDS, CAP), I32),
            sds((CAP, SHARDS), I32),
            sds((2 * DX, E), BF),
        ),
        (row_shard.transpose(1, 2, 0), local_row.T, bag_length.T, cross_down, cross_up),
        "index",
        scratch=[
            pltpu.VMEM((LOOK, 1, N), I32),
            pltpu.VMEM((LOOK, N), I32),
            pltpu.VMEM((F, N), I32),
            pltpu.VMEM((RANK, DX), BF),
            pltpu.SemaphoreType.DMA((5,)),
        ],
        flops=400_000_000,
        limit=56,
        far=range(5),
    )
    with jax.named_scope("gather_weights"):
        pack_all = lax.all_gather(pack, TPA, axis=0, tiled=False)
    ids = lax.all_to_all(ids, EMB, split_axis=0, concat_axis=0, tiled=True)
    (fetched,) = call(
        fetch_kernel, [sds((SHARDS, CAP, E), BF)], (ids, emb_table), "fetch", flops=1_300_000_000
    )
    returned = lax.all_to_all(fetched, EMB, split_axis=0, concat_axis=0, tiled=True)
    (pooled,) = call(
        pool_kernel,
        [sds((N, POOL), BF)],
        (returned, src),
        "pool",
        scratch=[pltpu.VMEM((BAGS, E), F32)],
        flops=1_060_000_000,
    )
    far = partner(pooled, "xh", 1)
    carried, send = call(
        main_kernel,
        (sds((N, POOL), F32), sds((SHARDS, CAP, E), BF)),
        (where, pooled, dense_input, pack_all, bias, head, label, feedback, src_t),
        "main",
        scratch=[
            pltpu.VMEM((DX, TP * RANK), BF),
            pltpu.VMEM((TP * RANK, DX), BF),
            pltpu.SemaphoreType.DMA((TP * (1 + BLOCKS),)),
        ],
        flops=10_000_000_000,
        limit=56,
        far=(3,),
    )
    far, again, send = lax.optimization_barrier((far, pooled, send))
    arrived = lax.all_to_all(send, EMB, split_axis=0, concat_axis=0, tiled=True)

    near, far_near = partner(again, "core", 1), partner(far, "core", 1)
    (part,) = call(
        grads_kernel,
        [sds((DP, SHARDS, CHUNK, E), BF)],
        (where, pooled, near, far, far_near, dense_input, pack_all, bias, head, label),
        "grads",
        scratch=[
            pltpu.VMEM((DENSE, DX), BF),
            pltpu.VMEM((DX, TP * RANK), BF),
            pltpu.VMEM((TP * RANK, DX), BF),
            pltpu.VMEM((TP, DENSE, RANK), BF),
            pltpu.VMEM((DX, RANK), BF),
            pltpu.VMEM((DX, RANK), BF),
            pltpu.SemaphoreType.DMA((TP * (1 + BLOCKS),)),
        ],
        flops=2_000_000_000,
        limit=56,
        far=(6,),
    )
    arrived, _ = lax.optimization_barrier((arrived, part))
    over_y = lax.psum_scatter(
        part.reshape(DP * SHARDS * CHUNK, E), "y", scatter_dimension=0, tiled=True
    )
    (row_grad,) = call(
        scatter_kernel,
        [sds((ROWS, E), BF)],
        (ids, arrived),
        "scatter",
        scratch=[pltpu.VMEM((ROWS, E), F32)],
        flops=1_300_000_000,
    )
    owners = ("y", "core")
    pieces = 2 * DP
    by_y = lax.all_to_all(row_grad, owners, split_axis=0, concat_axis=0, tiled=True)
    mine = jnp.sum(by_y.reshape(pieces, ROWS // pieces, E).astype(F32), axis=0)
    mine = (mine + partner(mine, "xh", 1)).astype(BF)
    over_y = over_y.reshape(SHARDS, CHUNK, E)
    over_all = lax.all_to_all(over_y, EMB, split_axis=0, concat_axis=0, tiled=True)
    spread = jnp.broadcast_to(mine[None], (pieces, ROWS // pieces, E)).reshape(ROWS, E)
    spread, over_all = lax.optimization_barrier((spread, over_all))
    full = lax.all_to_all(spread, owners, split_axis=0, concat_axis=0, tiled=True)
    full = full.astype(F32)
    accum_new = row_accum + full * full
    table_new = emb_table - LEARN * full / jnp.sqrt(accum_new)
    grads = jnp.sum(over_all.astype(F32), axis=0)
    grad_down = grads[0:GROUP]
    grad_up = grads[GROUP : 2 * GROUP].T
    grad_head = grads[2 * GROUP, 0:GROUP]
    grad_bias = grads[2 * GROUP, 16 : 16 + GROUP]

    return (table_new, accum_new, carried, grad_down, grad_up, grad_bias, grad_head)


def solution(mesh):
    fine = Mesh(mesh.devices.reshape(2, 8, 8, 2, 2), ("xl", "z", "y", "xh", "core"))
    dense = ("xl", "z", "y")
    every = ("xl", "z", "y", "xh", "core")
    in_specs = (
        P(EMB, None),
        P(EMB, None),
        P(dense, None),
        P(every, None, None),
        P(every, None),
        P(every, None),
        P(dense),
        P(every, None),
        P(None, TPA),
        P(TPA, None),
        P(),
        P(),
    )
    out_specs = (
        P(EMB, None),
        P(EMB, None),
        P(every, None),
        P(dense, TPA),
        P(TPA, dense),
        P(dense),
        P(dense),
    )
    return jax.shard_map(local, mesh=fine, in_specs=in_specs, out_specs=out_specs, check_vma=False)
```

```python
import jax
import jax.numpy as jnp
from jax import lax
from jax.experimental import pallas as pl
from jax.experimental.pallas import tpu as pltpu
from jax.sharding import Mesh, PartitionSpec as P

BF = jnp.bfloat16
F32 = jnp.float32
I32 = jnp.int32
E = 128
F = 13
BAG = 4
LOOK = F * BAG
N = 64
DENSE = 256
TP = 4
DP = 8
SHARDS = 16
CAP = 312
ROWS = 1024
DX = 1792
POOL = F * E
RANK = 128
GROUP = 14
CHUNK = 32
BLOCKS = DX // E
BAGS = N * F
LEARN = 0.5
EMB = ("xl", "z")
TPA = ("xh", "core")

VMEM = pl.BlockSpec(memory_space=pltpu.VMEM)
SMEM = pl.BlockSpec(memory_space=pltpu.SMEM)
ANY = pl.BlockSpec(memory_space=pl.ANY)


def iota(shape, axis):
    return lax.broadcasted_iota(I32, shape, axis)


def dot(a, b, ca=1, cb=0):
    return lax.dot_general(a, b, (((ca,), (cb,)), ((), ())), preferred_element_type=F32)


def call(kernel, outs, ins, name, scratch=(), limit=40, flops=0, far=()):
    nbytes = sum(x.size * x.dtype.itemsize for x in ins)
    return pl.pallas_call(
        kernel,
        out_shape=outs,
        in_specs=[SMEM if x.size < 8 else ANY if i in far else VMEM for i, x in enumerate(ins)],
        out_specs=[VMEM] * len(outs),
        scratch_shapes=scratch,
        compiler_params=pltpu.CompilerParams(vmem_limit_bytes=limit << 20),
        cost_estimate=pl.CostEstimate(flops=flops, bytes_accessed=nbytes, transcendentals=0),
        name=name,
    )(*ins)


def index_kernel(
    shard_hbm, row_hbm, len_hbm, down_hbm, up_hbm, ids_ref, src_ref, src_t_ref, pack_ref,
    shard_ref, row_ref, len_ref, up_ref, sems,
):
    moves = [(shard_hbm, shard_ref), (row_hbm, row_ref), (len_hbm, len_ref)]
    moves += [(down_hbm, pack_ref.at[pl.ds(0, DX), :]), (up_hbm, up_ref)]
    moves = [pltpu.make_async_copy(a, b, sems.at[i]) for i, (a, b) in enumerate(moves)]
    for move in moves:
        move.start()
    for move in moves[:3]:
        move.wait()

    def spread(values):
        parts = []
        for j in range(BAG):
            pick = (iota((F, LOOK), 1) == BAG * iota((F, LOOK), 0) + j).astype(F32).astype(BF)
            parts.append(dot(pick, values.astype(F32).astype(BF)))
        return jnp.concatenate(parts, axis=1)

    shard = spread(shard_ref[...].reshape(LOOK, N))
    rows = row_ref[...]
    row_lo, row_hi = spread(rows & 255), spread(rows >> 8)
    lens = len_ref[...].astype(F32)
    lens = jnp.concatenate([lens] * BAG, axis=1)
    wide = (F, BAG * N)
    lane = iota(wide, 1)
    usable = (lane >> 6).astype(F32) < lens
    bag = jnp.where(usable, iota(wide, 0) * N + (lane & (N - 1)) + 1, 0)
    bag_lo, bag_hi = (bag & 255).astype(F32), (bag & ~255).astype(F32)
    row_hi = row_hi * 256.0

    sq = (BAG * N, BAG * N)
    upper = (iota(sq, 0) < iota(sq, 1)).astype(F32).astype(BF)
    shards = iota((SHARDS, BAG * N), 0).astype(F32)
    slots = iota((CAP, BAG * N), 0).astype(F32)
    base = jnp.zeros((SHARDS, 1), F32)
    found = jnp.zeros((4 * SHARDS, CAP), F32)
    for f in range(F):
        hit = shards == shard[f : f + 1, :]
        one = jnp.where(hit, 1.0, 0.0)
        before = dot(one.astype(BF), upper) + base
        base = base + jnp.sum(one, axis=1, keepdims=True)
        rank = jnp.sum(one * before, axis=0, keepdims=True)
        place = jnp.where(slots == rank, 1.0, 0.0).astype(BF)
        values = [
            jnp.where(hit, v[f : f + 1, :], 0.0) for v in (row_lo, row_hi, bag_lo, bag_hi)
        ]
        found = found + dot(jnp.concatenate(values, axis=0).astype(BF), place, 1, 1)
    ids = found[0:SHARDS] + found[SHARDS : 2 * SHARDS]
    src = found[2 * SHARDS : 3 * SHARDS] + found[3 * SHARDS :] - 1.0
    ids_ref[...] = ids.astype(I32)
    src_ref[...] = src.astype(I32)
    src_t_ref[...] = jnp.transpose(src).astype(I32)
    for move in moves[3:]:
        move.wait()
    for j in range(BLOCKS):
        pack_ref[DX + j * E : DX + (j + 1) * E, :] = up_ref[:, j * E : (j + 1) * E]


def fetch_kernel(ids_ref, table_ref, out_ref):
    table = table_ref[...].astype(BF)
    cols = jnp.transpose(ids_ref[...].astype(F32))
    lanes = iota((CAP, ROWS), 1).astype(F32)
    for s in range(SHARDS):
        pick = jnp.where(cols[:, s : s + 1] == lanes, 1.0, 0.0).astype(BF)
        out_ref[s] = dot(pick, table).astype(BF)


def start_weights(pack_ref, down_ref, up_ref, sems):
    moves = []
    for k in range(TP):
        block = pl.ds(k * RANK, RANK)
        moves.append((pack_ref.at[k, pl.ds(0, DX), :], down_ref.at[:, block]))
        for j in range(BLOCKS):
            lanes = pl.ds(j * E, E)
            moves.append((pack_ref.at[k, pl.ds(DX + j * E, E), :], up_ref.at[block, lanes]))
    moves = [pltpu.make_async_copy(a, b, sems.at[i]) for i, (a, b) in enumerate(moves)]
    for move in moves:
        move.start()
    return moves


def forward(x, down, up, bias, head, labels):
    hidden = dot(x, down).astype(BF)
    crossed = dot(hidden, up)
    xf = x.astype(F32)
    x_next = xf * (crossed + bias) + xf
    logits = jnp.sum(x_next * head, axis=1, keepdims=True)
    grad_logit = jax.nn.sigmoid(logits) - labels.astype(F32)
    grad_next = grad_logit * head
    return hidden, crossed, xf, x_next, grad_logit, grad_next, grad_next * xf


def pool_kernel(rows_ref, src_ref, pack_ref, pooled_ref, down_ref, up_ref, acc_ref, sems):
    moves = start_weights(pack_ref, down_ref, up_ref, sems)
    bags = iota((BAGS, CAP), 0)
    for s in range(SHARDS):
        pick = jnp.where(bags == src_ref[s : s + 1, :], 1.0, 0.0).astype(BF)
        term = dot(pick, rows_ref[s])
        if s == 0:
            acc_ref[...] = term
        else:
            acc_ref[...] += term
    for f in range(F):
        pooled_ref[:, f * E : (f + 1) * E] = acc_ref[f * N : (f + 1) * N, :].astype(BF)
    for move in moves:
        move.wait()


def main_kernel(
    where_ref, pooled_ref, dense_ref, down_ref, up_ref, bias_ref, head_ref, label_ref, feedback_ref,
    src_t_ref, carried_ref, send_ref,
):
    first = pl.multiple_of(where_ref[0] * N, N)
    x = jnp.concatenate([dense_ref[pl.ds(first, N), :], pooled_ref[...]], axis=1)
    up, bias, head = up_ref[...], bias_ref[...], head_ref[...]
    _, crossed, _, _, _, grad_next, cross = forward(
        x, down_ref[...], up, bias, head, label_ref[pl.ds(first, N), :]
    )
    grad_cross = cross.astype(BF)
    grad_hidden = dot(grad_cross, up, 1, 1).astype(BF)
    back = dot(grad_hidden, down_ref[E:, :], 1, 1)
    carried = grad_next[:, E:] * (crossed[:, E:] + bias[:, E:] + 1.0) + back + feedback_ref[...]
    carried_ref[...] = carried
    sent = carried.astype(BF)
    by_bag = jnp.concatenate([sent[:, f * E : (f + 1) * E] for f in range(F)], axis=0)
    bags = iota((CAP, BAGS), 1)
    for s in range(SHARDS):
        pick = jnp.where(src_t_ref[:, s : s + 1] == bags, 1.0, 0.0).astype(BF)
        send_ref[s] = dot(pick, by_bag).astype(BF)


def grads_kernel(
    where_ref, s0_ref, s1_ref, s2_ref, s3_ref, dense_ref, down_ref, up_ref, bias_ref, head_ref,
    label_ref, out_ref, x_ref, hidden_ref, down_grad_ref, up_grad_ref,
):
    t = where_ref[0]
    x_ref[:, 0:E] = dense_ref[...]
    for m, ref in enumerate((s0_ref, s1_ref, s2_ref, s3_ref)):
        x_ref[pl.ds(pl.multiple_of((t ^ m) * N, N), N), E:] = ref[...]
    x = x_ref[...]
    hidden, _, _, x_next, grad_logit, _, cross = forward(
        x, down_ref[...], up_ref[...], bias_ref[...], head_ref[...], label_ref[...]
    )
    for k in range(TP):
        hidden_ref[k] = hidden[:, k * RANK : (k + 1) * RANK]
    hidden = hidden_ref[t]
    up = up_ref[pl.ds(pl.multiple_of(t * RANK, RANK), RANK), :]
    grad_cross = cross.astype(BF)
    grad_bias = jnp.sum(cross, axis=0, keepdims=True)
    grad_head = jnp.sum(grad_logit * x_next, axis=0, keepdims=True)
    grad_hidden = dot(grad_cross, up, 1, 1).astype(BF)
    down_grad_ref[...] = dot(x, grad_hidden, 0, 0).astype(BF)
    up_grad_ref[...] = dot(grad_cross, hidden, 0, 0).astype(BF)

    groups = DX // GROUP
    r = iota((groups, DX), 1) - GROUP * iota((groups, DX), 0)
    own = (r >= 0) & (r < GROUP)
    rows = iota((DX, E), 0)
    rest14 = rows - GROUP * jnp.floor((rows.astype(F32) + 0.5) * (1.0 / GROUP)).astype(I32)
    small = jnp.zeros((groups, E), F32)
    for p, v in enumerate((grad_head, grad_bias)):
        spread = jnp.where(own, v, 0.0).astype(BF)
        lanes = jnp.where(iota((DX, E), 1) == rest14 + 16 * p, 1.0, 0.0).astype(BF)
        small = small + dot(spread, lanes)

    block = DP * GROUP
    q = (DP * CHUNK, 2 * block + 32)
    d, rho, col = iota(q, 0) >> 5, iota(q, 0) & 31, iota(q, 1)
    want = jnp.where(
        rho < GROUP,
        GROUP * d + rho,
        jnp.where(
            rho < 2 * GROUP,
            block + GROUP * d + rho - GROUP,
            jnp.where(rho == 2 * GROUP, 2 * block + d, -1),
        ),
    )
    select = jnp.where(col == want, 1.0, 0.0).astype(BF)
    for e in range(SHARDS):
        part = jnp.concatenate([small[DP * e : DP * e + DP], jnp.zeros((24, E), F32)], axis=0)
        block_rows = jnp.concatenate(
            [
                down_grad_ref[block * e : block * (e + 1), :],
                up_grad_ref[block * e : block * (e + 1), :],
                part.astype(BF),
            ],
            axis=0,
        )
        got = dot(select, block_rows).astype(BF)
        w = where_ref[2] ^ e
        place = ((w >> 3) & 1) * 8 + (w & 1) * 4 + ((w >> 1) & 3)
        for k in range(DP):
            out_ref[k, place] = got[CHUNK * k : CHUNK * (k + 1)]


def scatter_kernel(ids_ref, rows_ref, out_ref, acc_ref):
    rows = iota((ROWS, CAP), 0)
    for s in range(SHARDS):
        pick = jnp.where(rows == ids_ref[s : s + 1, :], 1.0, 0.0).astype(BF)
        term = dot(pick, rows_ref[s])
        if s == 0:
            acc_ref[...] = term
        else:
            acc_ref[...] += term
    out_ref[...] = acc_ref[...].astype(BF)


def partner(value, axes, mask):
    size = lax.axis_size(axes)
    return lax.ppermute(value, axes, [(i, i ^ mask) for i in range(size)])


def sds(shape, dtype):
    return jax.ShapeDtypeStruct(shape, dtype)


def local(
    emb_table, row_accum, dense_input, row_shard, local_row, bag_length, labels, feedback,
    cross_down, cross_up, cross_bias, head_weight,
):
    bias, head = cross_bias.reshape(1, DX), head_weight.reshape(1, DX)
    label = labels.reshape(DENSE, 1)
    where = jnp.stack([lax.axis_index(TPA), lax.axis_index("y"), lax.axis_index(EMB)]).astype(I32)
    ids, src, src_t, pack = call(
        index_kernel,
        (
            sds((SHARDS, CAP), I32),
            sds((SHARDS, CAP), I32),
            sds((CAP, SHARDS), I32),
            sds((2 * DX, E), BF),
        ),
        (row_shard.transpose(1, 2, 0), local_row.T, bag_length.T, cross_down, cross_up),
        "index",
        scratch=[
            pltpu.VMEM((LOOK, 1, N), I32),
            pltpu.VMEM((LOOK, N), I32),
            pltpu.VMEM((F, N), I32),
            pltpu.VMEM((RANK, DX), BF),
            pltpu.SemaphoreType.DMA((5,)),
        ],
        flops=400_000_000,
        limit=56,
        far=range(5),
    )
    with jax.named_scope("gather_weights"):
        pack_all = lax.all_gather(pack, TPA, axis=0, tiled=False)
    ids = lax.all_to_all(ids, EMB, split_axis=0, concat_axis=0, tiled=True)
    (fetched,) = call(
        fetch_kernel, [sds((SHARDS, CAP, E), BF)], (ids, emb_table), "fetch", flops=1_300_000_000
    )
    returned = lax.all_to_all(fetched, EMB, split_axis=0, concat_axis=0, tiled=True)
    pooled, down_all, up_all = call(
        pool_kernel,
        [sds((N, POOL), BF), sds((DX, TP * RANK), BF), sds((TP * RANK, DX), BF)],
        (returned, src, pack_all),
        "pool",
        scratch=[
            pltpu.VMEM((BAGS, E), F32),
            pltpu.SemaphoreType.DMA((TP * (1 + BLOCKS),)),
        ],
        flops=1_060_000_000,
        limit=47,
        far=(2,),
    )
    far = partner(pooled, "xh", 1)
    carried, send = call(
        main_kernel,
        (sds((N, POOL), F32), sds((SHARDS, CAP, E), BF)),
        (where, pooled, dense_input, down_all, up_all, bias, head, label, feedback, src_t),
        "main",
        flops=10_000_000_000,
        limit=40,
    )
    far, again, send = lax.optimization_barrier((far, pooled, send))
    arrived = lax.all_to_all(send, EMB, split_axis=0, concat_axis=0, tiled=True)

    near, far_near = partner(again, "core", 1), partner(far, "core", 1)
    (part,) = call(
        grads_kernel,
        [sds((DP, SHARDS, CHUNK, E), BF)],
        (where, pooled, near, far, far_near, dense_input, down_all, up_all, bias, head, label),
        "grads",
        scratch=[
            pltpu.VMEM((DENSE, DX), BF),
            pltpu.VMEM((TP, DENSE, RANK), BF),
            pltpu.VMEM((DX, RANK), BF),
            pltpu.VMEM((DX, RANK), BF),
        ],
        flops=2_000_000_000,
        limit=40,
    )
    arrived, _ = lax.optimization_barrier((arrived, part))
    over_y = lax.psum_scatter(
        part.reshape(DP * SHARDS * CHUNK, E), "y", scatter_dimension=0, tiled=True
    )
    (row_grad,) = call(
        scatter_kernel,
        [sds((ROWS, E), BF)],
        (ids, arrived),
        "scatter",
        scratch=[pltpu.VMEM((ROWS, E), F32)],
        flops=1_300_000_000,
    )
    owners = ("y", "core")
    pieces = 2 * DP
    by_y = lax.all_to_all(row_grad, owners, split_axis=0, concat_axis=0, tiled=True)
    mine = jnp.sum(by_y.reshape(pieces, ROWS // pieces, E).astype(F32), axis=0)
    mine = (mine + partner(mine, "xh", 1)).astype(BF)
    over_y = over_y.reshape(SHARDS, CHUNK, E)
    pairs = [over_y[0:4].astype(F32)] + [
        partner(over_y[4 * c : 4 * c + 4], EMB, mask).astype(F32)
        for c, mask in ((1, 1), (2, 8), (3, 9))
    ]
    pairs = (pairs[0] + pairs[1]) + (pairs[2] + pairs[3])
    spread = jnp.broadcast_to(mine[None], (pieces, ROWS // pieces, E)).reshape(ROWS, E)
    last = [pairs[0]] + [pairs[i].astype(BF) for i in (1, 2, 3)]
    spread, *last = lax.optimization_barrier((spread, *last))
    full = lax.all_to_all(spread, owners, split_axis=0, concat_axis=0, tiled=True)
    last = [last[0]] + [partner(last[i], EMB, 2 * i).astype(F32) for i in (1, 2, 3)]
    grads = (last[0] + last[1]) + (last[2] + last[3])
    full = full.astype(F32)
    accum_new = row_accum + full * full
    table_new = emb_table - LEARN * full / jnp.sqrt(accum_new)
    grad_down = grads[0:GROUP]
    grad_up = grads[GROUP : 2 * GROUP].T
    grad_head = grads[2 * GROUP, 0:GROUP]
    grad_bias = grads[2 * GROUP, 16 : 16 + GROUP]

    return (table_new, accum_new, carried, grad_down, grad_up, grad_bias, grad_head)


def solution(mesh):
    fine = Mesh(mesh.devices.reshape(2, 8, 8, 2, 2), ("xl", "z", "y", "xh", "core"))
    dense = ("xl", "z", "y")
    every = ("xl", "z", "y", "xh", "core")
    in_specs = (
        P(EMB, None),
        P(EMB, None),
        P(dense, None),
        P(every, None, None),
        P(every, None),
        P(every, None),
        P(dense),
        P(every, None),
        P(None, TPA),
        P(TPA, None),
        P(),
        P(),
    )
    out_specs = (
        P(EMB, None),
        P(EMB, None),
        P(every, None),
        P(dense, TPA),
        P(TPA, dense),
        P(dense),
        P(dense),
    )
    return jax.shard_map(local, mesh=fine, in_specs=in_specs, out_specs=out_specs, check_vma=False)
```

```python
import jax
import jax.numpy as jnp
from jax import lax
from jax.experimental import pallas as pl
from jax.experimental.pallas import tpu as pltpu
from jax.sharding import Mesh, PartitionSpec as P

BF = jnp.bfloat16
F32 = jnp.float32
I32 = jnp.int32
E = 128
F = 13
BAG = 4
LOOK = F * BAG
N = 64
DENSE = 256
TP = 4
DP = 8
SHARDS = 16
CAP = 312
ROWS = 1024
DX = 1792
POOL = F * E
RANK = 128
GROUP = 14
CHUNK = 32
BLOCKS = DX // E
BAGS = N * F
LEARN = 0.5
EMB = ("xl", "z")
TPA = ("xh", "core")

VMEM = pl.BlockSpec(memory_space=pltpu.VMEM)
SMEM = pl.BlockSpec(memory_space=pltpu.SMEM)
ANY = pl.BlockSpec(memory_space=pl.ANY)


def iota(shape, axis):
    return lax.broadcasted_iota(I32, shape, axis)


def dot(a, b, ca=1, cb=0):
    return lax.dot_general(a, b, (((ca,), (cb,)), ((), ())), preferred_element_type=F32)


def call(kernel, outs, ins, name, scratch=(), limit=40, flops=0, far=()):
    nbytes = sum(x.size * x.dtype.itemsize for x in ins)
    return pl.pallas_call(
        kernel,
        out_shape=outs,
        in_specs=[SMEM if x.size < 8 else ANY if i in far else VMEM for i, x in enumerate(ins)],
        out_specs=[VMEM] * len(outs),
        scratch_shapes=scratch,
        compiler_params=pltpu.CompilerParams(vmem_limit_bytes=limit << 20),
        cost_estimate=pl.CostEstimate(flops=flops, bytes_accessed=nbytes, transcendentals=0),
        name=name,
    )(*ins)


def index_kernel(
    shard_hbm, row_hbm, len_hbm, down_hbm, up_hbm, ids_ref, src_ref, src_t_ref, pack_ref,
    shard_ref, row_ref, len_ref, up_ref, sems,
):
    moves = [(shard_hbm, shard_ref), (row_hbm, row_ref), (len_hbm, len_ref)]
    moves += [(down_hbm, pack_ref.at[pl.ds(0, DX), :]), (up_hbm, up_ref)]
    moves = [pltpu.make_async_copy(a, b, sems.at[i]) for i, (a, b) in enumerate(moves)]
    for move in moves:
        move.start()
    for move in moves[:3]:
        move.wait()

    def spread(values):
        parts = []
        for j in range(BAG):
            pick = (iota((F, LOOK), 1) == BAG * iota((F, LOOK), 0) + j).astype(F32).astype(BF)
            parts.append(dot(pick, values.astype(F32).astype(BF)))
        return jnp.concatenate(parts, axis=1)

    shard = spread(shard_ref[...].reshape(LOOK, N))
    rows = row_ref[...]
    row_lo, row_hi = spread(rows & 255), spread(rows >> 8)
    lens = len_ref[...].astype(F32)
    lens = jnp.concatenate([lens] * BAG, axis=1)
    wide = (F, BAG * N)
    lane = iota(wide, 1)
    usable = (lane >> 6).astype(F32) < lens
    bag = jnp.where(usable, iota(wide, 0) * N + (lane & (N - 1)) + 1, 0)
    bag_lo, bag_hi = (bag & 255).astype(F32), (bag & ~255).astype(F32)
    row_hi = row_hi * 256.0

    sq = (BAG * N, BAG * N)
    upper = (iota(sq, 0) < iota(sq, 1)).astype(F32).astype(BF)
    shards = iota((SHARDS, BAG * N), 0).astype(F32)
    slots = iota((CAP, BAG * N), 0).astype(F32)
    base = jnp.zeros((SHARDS, 1), F32)
    found = jnp.zeros((4 * SHARDS, CAP), F32)
    for f in range(F):
        hit = shards == shard[f : f + 1, :]
        one = jnp.where(hit, 1.0, 0.0)
        before = dot(one.astype(BF), upper) + base
        base = base + jnp.sum(one, axis=1, keepdims=True)
        rank = jnp.sum(one * before, axis=0, keepdims=True)
        place = jnp.where(slots == rank, 1.0, 0.0).astype(BF)
        values = [
            jnp.where(hit, v[f : f + 1, :], 0.0) for v in (row_lo, row_hi, bag_lo, bag_hi)
        ]
        found = found + dot(jnp.concatenate(values, axis=0).astype(BF), place, 1, 1)
    ids = found[0:SHARDS] + found[SHARDS : 2 * SHARDS]
    src = found[2 * SHARDS : 3 * SHARDS] + found[3 * SHARDS :] - 1.0
    ids_ref[...] = ids.astype(I32)
    src_ref[...] = src.astype(I32)
    src_t_ref[...] = jnp.transpose(src).astype(I32)
    for move in moves[3:]:
        move.wait()
    for j in range(BLOCKS):
        pack_ref[DX + j * E : DX + (j + 1) * E, :] = up_ref[:, j * E : (j + 1) * E]


def fetch_kernel(ids_ref, table_ref, out_ref):
    table = table_ref[...].astype(BF)
    cols = jnp.transpose(ids_ref[...].astype(F32))
    lanes = iota((CAP, ROWS), 1).astype(F32)
    for s in range(SHARDS):
        pick = jnp.where(cols[:, s : s + 1] == lanes, 1.0, 0.0).astype(BF)
        out_ref[s] = dot(pick, table).astype(BF)


def arrange(pack_ref, down_ref, up_ref):
    for k in range(TP):
        block = slice(k * RANK, (k + 1) * RANK)
        down_ref[:, block] = pack_ref[k, 0:DX, :]
        for j in range(BLOCKS):
            rows = slice(DX + j * E, DX + (j + 1) * E)
            up_ref[block, j * E : (j + 1) * E] = pack_ref[k, rows, :]


def forward(x, down, up, bias, head, labels):
    hidden = dot(x, down).astype(BF)
    crossed = dot(hidden, up)
    xf = x.astype(F32)
    x_next = xf * (crossed + bias) + xf
    logits = jnp.sum(x_next * head, axis=1, keepdims=True)
    grad_logit = jax.nn.sigmoid(logits) - labels.astype(F32)
    grad_next = grad_logit * head
    return hidden, crossed, xf, x_next, grad_logit, grad_next, grad_next * xf


def pool_kernel(rows_ref, src_ref, pack_hbm, pooled_ref, pack_ref, acc_ref, sems):
    moves = [
        pltpu.make_async_copy(pack_hbm.at[k], pack_ref.at[k], sems.at[k]) for k in range(TP)
    ]
    for move in moves:
        move.start()
    bags = iota((BAGS, CAP), 0)
    for s in range(SHARDS):
        pick = jnp.where(bags == src_ref[s : s + 1, :], 1.0, 0.0).astype(BF)
        term = dot(pick, rows_ref[s])
        if s == 0:
            acc_ref[...] = term
        else:
            acc_ref[...] += term
    for f in range(F):
        pooled_ref[:, f * E : (f + 1) * E] = acc_ref[f * N : (f + 1) * N, :].astype(BF)
    for move in moves:
        move.wait()


def main_kernel(
    where_ref, pooled_ref, dense_ref, pack_ref, bias_ref, head_ref, label_ref, feedback_ref,
    src_t_ref, carried_ref, send_ref, down_ref, up_ref,
):
    arrange(pack_ref, down_ref, up_ref)
    first = pl.multiple_of(where_ref[0] * N, N)
    x = jnp.concatenate([dense_ref[pl.ds(first, N), :], pooled_ref[...]], axis=1)
    up, bias, head = up_ref[...], bias_ref[...], head_ref[...]
    _, crossed, _, _, _, grad_next, cross = forward(
        x, down_ref[...], up, bias, head, label_ref[pl.ds(first, N), :]
    )
    grad_cross = cross.astype(BF)
    grad_hidden = dot(grad_cross, up, 1, 1).astype(BF)
    back = dot(grad_hidden, down_ref[E:, :], 1, 1)
    carried = grad_next[:, E:] * (crossed[:, E:] + bias[:, E:] + 1.0) + back + feedback_ref[...]
    carried_ref[...] = carried
    sent = carried.astype(BF)
    by_bag = jnp.concatenate([sent[:, f * E : (f + 1) * E] for f in range(F)], axis=0)
    bags = iota((CAP, BAGS), 1)
    for s in range(SHARDS):
        pick = jnp.where(src_t_ref[:, s : s + 1] == bags, 1.0, 0.0).astype(BF)
        send_ref[s] = dot(pick, by_bag).astype(BF)


def grads_kernel(
    where_ref, s0_ref, s1_ref, s2_ref, s3_ref, dense_ref, pack_ref, bias_ref, head_ref, label_ref,
    out_ref, x_ref, hidden_ref, down_grad_ref, up_grad_ref, down_ref, up_ref,
):
    arrange(pack_ref, down_ref, up_ref)
    t = where_ref[0]
    x_ref[:, 0:E] = dense_ref[...]
    for m, ref in enumerate((s0_ref, s1_ref, s2_ref, s3_ref)):
        x_ref[pl.ds(pl.multiple_of((t ^ m) * N, N), N), E:] = ref[...]
    x = x_ref[...]
    hidden, _, _, x_next, grad_logit, _, cross = forward(
        x, down_ref[...], up_ref[...], bias_ref[...], head_ref[...], label_ref[...]
    )
    for k in range(TP):
        hidden_ref[k] = hidden[:, k * RANK : (k + 1) * RANK]
    hidden = hidden_ref[t]
    up = up_ref[pl.ds(pl.multiple_of(t * RANK, RANK), RANK), :]
    grad_cross = cross.astype(BF)
    grad_bias = jnp.sum(cross, axis=0, keepdims=True)
    grad_head = jnp.sum(grad_logit * x_next, axis=0, keepdims=True)
    grad_hidden = dot(grad_cross, up, 1, 1).astype(BF)
    down_grad_ref[...] = dot(x, grad_hidden, 0, 0).astype(BF)
    up_grad_ref[...] = dot(grad_cross, hidden, 0, 0).astype(BF)

    groups = DX // GROUP
    r = iota((groups, DX), 1) - GROUP * iota((groups, DX), 0)
    own = (r >= 0) & (r < GROUP)
    rows = iota((DX, E), 0)
    rest14 = rows - GROUP * jnp.floor((rows.astype(F32) + 0.5) * (1.0 / GROUP)).astype(I32)
    small = jnp.zeros((groups, E), F32)
    for p, v in enumerate((grad_head, grad_bias)):
        spread = jnp.where(own, v, 0.0).astype(BF)
        lanes = jnp.where(iota((DX, E), 1) == rest14 + 16 * p, 1.0, 0.0).astype(BF)
        small = small + dot(spread, lanes)

    block = DP * GROUP
    q = (DP * CHUNK, 2 * block + 32)
    d, rho, col = iota(q, 0) >> 5, iota(q, 0) & 31, iota(q, 1)
    want = jnp.where(
        rho < GROUP,
        GROUP * d + rho,
        jnp.where(
            rho < 2 * GROUP,
            block + GROUP * d + rho - GROUP,
            jnp.where(rho == 2 * GROUP, 2 * block + d, -1),
        ),
    )
    select = jnp.where(col == want, 1.0, 0.0).astype(BF)
    for e in range(SHARDS):
        part = jnp.concatenate([small[DP * e : DP * e + DP], jnp.zeros((24, E), F32)], axis=0)
        block_rows = jnp.concatenate(
            [
                down_grad_ref[block * e : block * (e + 1), :],
                up_grad_ref[block * e : block * (e + 1), :],
                part.astype(BF),
            ],
            axis=0,
        )
        got = dot(select, block_rows).astype(BF)
        w = where_ref[2] ^ e
        place = ((w >> 3) & 1) * 8 + (w & 1) * 4 + ((w >> 1) & 3)
        for k in range(DP):
            out_ref[k, place] = got[CHUNK * k : CHUNK * (k + 1)]


def scatter_kernel(ids_ref, rows_ref, out_ref, acc_ref):
    rows = iota((ROWS, CAP), 0)
    for s in range(SHARDS):
        pick = jnp.where(rows == ids_ref[s : s + 1, :], 1.0, 0.0).astype(BF)
        term = dot(pick, rows_ref[s])
        if s == 0:
            acc_ref[...] = term
        else:
            acc_ref[...] += term
    out_ref[...] = acc_ref[...].astype(BF)


def partner(value, axes, mask):
    size = lax.axis_size(axes)
    return lax.ppermute(value, axes, [(i, i ^ mask) for i in range(size)])


def sds(shape, dtype):
    return jax.ShapeDtypeStruct(shape, dtype)


def local(
    emb_table, row_accum, dense_input, row_shard, local_row, bag_length, labels, feedback,
    cross_down, cross_up, cross_bias, head_weight,
):
    bias, head = cross_bias.reshape(1, DX), head_weight.reshape(1, DX)
    label = labels.reshape(DENSE, 1)
    where = jnp.stack([lax.axis_index(TPA), lax.axis_index("y"), lax.axis_index(EMB)]).astype(I32)
    ids, src, src_t, pack = call(
        index_kernel,
        (
            sds((SHARDS, CAP), I32),
            sds((SHARDS, CAP), I32),
            sds((CAP, SHARDS), I32),
            sds((2 * DX, E), BF),
        ),
        (row_shard.transpose(1, 2, 0), local_row.T, bag_length.T, cross_down, cross_up),
        "index",
        scratch=[
            pltpu.VMEM((LOOK, 1, N), I32),
            pltpu.VMEM((LOOK, N), I32),
            pltpu.VMEM((F, N), I32),
            pltpu.VMEM((RANK, DX), BF),
            pltpu.SemaphoreType.DMA((5,)),
        ],
        flops=400_000_000,
        limit=56,
        far=range(5),
    )
    with jax.named_scope("gather_weights"):
        pack_all = lax.all_gather(pack, TPA, axis=0, tiled=False)
    ids = lax.all_to_all(ids, EMB, split_axis=0, concat_axis=0, tiled=True)
    (fetched,) = call(
        fetch_kernel, [sds((SHARDS, CAP, E), BF)], (ids, emb_table), "fetch", flops=1_300_000_000
    )
    returned = lax.all_to_all(fetched, EMB, split_axis=0, concat_axis=0, tiled=True)
    pooled, weights = call(
        pool_kernel,
        [sds((N, POOL), BF), sds((TP, 2 * DX, E), BF)],
        (returned, src, pack_all),
        "pool",
        scratch=[
            pltpu.VMEM((BAGS, E), F32),
            pltpu.SemaphoreType.DMA((TP,)),
        ],
        flops=1_060_000_000,
        limit=47,
        far=(2,),
    )
    far = partner(pooled, "xh", 1)
    carried, send = call(
        main_kernel,
        (sds((N, POOL), F32), sds((SHARDS, CAP, E), BF)),
        (where, pooled, dense_input, weights, bias, head, label, feedback, src_t),
        "main",
        scratch=[pltpu.VMEM((DX, TP * RANK), BF), pltpu.VMEM((TP * RANK, DX), BF)],
        flops=10_000_000_000,
        limit=40,
    )
    far, again, send = lax.optimization_barrier((far, pooled, send))
    arrived = lax.all_to_all(send, EMB, split_axis=0, concat_axis=0, tiled=True)

    near, far_near = partner(again, "core", 1), partner(far, "core", 1)
    (part,) = call(
        grads_kernel,
        [sds((DP, SHARDS, CHUNK, E), BF)],
        (where, pooled, near, far, far_near, dense_input, weights, bias, head, label),
        "grads",
        scratch=[
            pltpu.VMEM((DENSE, DX), BF),
            pltpu.VMEM((TP, DENSE, RANK), BF),
            pltpu.VMEM((DX, RANK), BF),
            pltpu.VMEM((DX, RANK), BF),
            pltpu.VMEM((DX, TP * RANK), BF),
            pltpu.VMEM((TP * RANK, DX), BF),
        ],
        flops=2_000_000_000,
        limit=40,
    )
    arrived, _ = lax.optimization_barrier((arrived, part))
    over_y = lax.psum_scatter(
        part.reshape(DP * SHARDS * CHUNK, E), "y", scatter_dimension=0, tiled=True
    )
    (row_grad,) = call(
        scatter_kernel,
        [sds((ROWS, E), BF)],
        (ids, arrived),
        "scatter",
        scratch=[pltpu.VMEM((ROWS, E), F32)],
        flops=1_300_000_000,
    )
    owners = ("y", "core")
    pieces = 2 * DP
    by_y = lax.all_to_all(row_grad, owners, split_axis=0, concat_axis=0, tiled=True)
    mine = jnp.sum(by_y.reshape(pieces, ROWS // pieces, E).astype(F32), axis=0)
    mine = (mine + partner(mine, "xh", 1)).astype(BF)
    spread = jnp.broadcast_to(mine[None], (pieces, ROWS // pieces, E)).reshape(ROWS, E)
    spread, over_y = lax.optimization_barrier((spread, over_y))
    full = lax.all_to_all(spread, owners, split_axis=0, concat_axis=0, tiled=True)
    over_y = over_y.reshape(SHARDS, CHUNK, E)
    pairs = [over_y[0:4].astype(F32)] + [
        partner(over_y[4 * c : 4 * c + 4], EMB, mask).astype(F32)
        for c, mask in ((1, 1), (2, 8), (3, 9))
    ]
    pairs = (pairs[0] + pairs[1]) + (pairs[2] + pairs[3])
    last = [pairs[0]] + [
        partner(pairs[i].astype(BF), EMB, 2 * i).astype(F32) for i in (1, 2, 3)
    ]
    grads = (last[0] + last[1]) + (last[2] + last[3])
    full = full.astype(F32)
    accum_new = row_accum + full * full
    table_new = emb_table - LEARN * full / jnp.sqrt(accum_new)
    grad_down = grads[0:GROUP]
    grad_up = grads[GROUP : 2 * GROUP].T
    grad_head = grads[2 * GROUP, 0:GROUP]
    grad_bias = grads[2 * GROUP, 16 : 16 + GROUP]

    return (table_new, accum_new, carried, grad_down, grad_up, grad_bias, grad_head)


def solution(mesh):
    fine = Mesh(mesh.devices.reshape(2, 8, 8, 2, 2), ("xl", "z", "y", "xh", "core"))
    dense = ("xl", "z", "y")
    every = ("xl", "z", "y", "xh", "core")
    in_specs = (
        P(EMB, None),
        P(EMB, None),
        P(dense, None),
        P(every, None, None),
        P(every, None),
        P(every, None),
        P(dense),
        P(every, None),
        P(None, TPA),
        P(TPA, None),
        P(),
        P(),
    )
    out_specs = (
        P(EMB, None),
        P(EMB, None),
        P(every, None),
        P(dense, TPA),
        P(TPA, dense),
        P(dense),
        P(dense),
    )
    return jax.shard_map(local, mesh=fine, in_specs=in_specs, out_specs=out_specs, check_vma=False)
```

```python
import jax
import jax.numpy as jnp
from jax import lax
from jax.experimental import pallas as pl
from jax.experimental.pallas import tpu as pltpu
from jax.sharding import Mesh, PartitionSpec as P

BF = jnp.bfloat16
F32 = jnp.float32
I32 = jnp.int32
E = 128
F = 13
BAG = 4
LOOK = F * BAG
N = 64
DENSE = 256
TP = 4
DP = 8
SHARDS = 16
CAP = 312
ROWS = 1024
DX = 1792
POOL = F * E
RANK = 128
GROUP = 14
CHUNK = 32
BLOCKS = DX // E
BAGS = N * F
QUAD = 4
LEARN = 0.5
EMB = ("xl", "z")
TPA = ("xh", "core")

VMEM = pl.BlockSpec(memory_space=pltpu.VMEM)
SMEM = pl.BlockSpec(memory_space=pltpu.SMEM)
ANY = pl.BlockSpec(memory_space=pl.ANY)


def iota(shape, axis):
    return lax.broadcasted_iota(I32, shape, axis)


def dot(a, b, ca=1, cb=0):
    return lax.dot_general(a, b, (((ca,), (cb,)), ((), ())), preferred_element_type=F32)


def call(kernel, outs, ins, name, scratch=(), limit=40, flops=0, far=()):
    nbytes = sum(x.size * x.dtype.itemsize for x in ins)
    return pl.pallas_call(
        kernel,
        out_shape=outs,
        in_specs=[SMEM if x.size < 8 else ANY if i in far else VMEM for i, x in enumerate(ins)],
        out_specs=[VMEM] * len(outs),
        scratch_shapes=scratch,
        compiler_params=pltpu.CompilerParams(vmem_limit_bytes=limit << 20),
        cost_estimate=pl.CostEstimate(flops=flops, bytes_accessed=nbytes, transcendentals=0),
        name=name,
    )(*ins)


def index_kernel(
    shard_hbm, row_hbm, len_hbm, down_hbm, up_hbm, ids_ref, src_ref, src_t_ref, pack_ref,
    shard_ref, row_ref, len_ref, up_ref, sems,
):
    moves = [(shard_hbm, shard_ref), (row_hbm, row_ref), (len_hbm, len_ref)]
    moves += [(down_hbm, pack_ref.at[pl.ds(0, DX), :]), (up_hbm, up_ref)]
    moves = [pltpu.make_async_copy(a, b, sems.at[i]) for i, (a, b) in enumerate(moves)]
    for move in moves:
        move.start()
    for move in moves[:3]:
        move.wait()

    def spread(values):
        parts = []
        for j in range(BAG):
            pick = (iota((F, LOOK), 1) == BAG * iota((F, LOOK), 0) + j).astype(F32).astype(BF)
            parts.append(dot(pick, values.astype(F32).astype(BF)))
        return jnp.concatenate(parts, axis=1)

    shard = spread(shard_ref[...].reshape(LOOK, N))
    rows = row_ref[...]
    row_lo, row_hi = spread(rows & 255), spread(rows >> 8)
    lens = len_ref[...].astype(F32)
    lens = jnp.concatenate([lens] * BAG, axis=1)
    wide = (F, BAG * N)
    lane = iota(wide, 1)
    usable = (lane >> 6).astype(F32) < lens
    bag = jnp.where(usable, iota(wide, 0) * N + (lane & (N - 1)) + 1, 0)
    bag_lo, bag_hi = (bag & 255).astype(F32), (bag & ~255).astype(F32)
    row_hi = row_hi * 256.0

    sq = (BAG * N, BAG * N)
    upper = (iota(sq, 0) < iota(sq, 1)).astype(F32).astype(BF)
    shards = iota((SHARDS, BAG * N), 0).astype(F32)
    slots = iota((CAP, BAG * N), 0).astype(F32)
    base = jnp.zeros((SHARDS, 1), F32)
    found = jnp.zeros((4 * SHARDS, CAP), F32)
    for f in range(F):
        hit = shards == shard[f : f + 1, :]
        one = jnp.where(hit, 1.0, 0.0)
        before = dot(one.astype(BF), upper) + base
        base = base + jnp.sum(one, axis=1, keepdims=True)
        rank = jnp.sum(one * before, axis=0, keepdims=True)
        place = jnp.where(slots == rank, 1.0, 0.0).astype(BF)
        values = [
            jnp.where(hit, v[f : f + 1, :], 0.0) for v in (row_lo, row_hi, bag_lo, bag_hi)
        ]
        found = found + dot(jnp.concatenate(values, axis=0).astype(BF), place, 1, 1)
    ids = found[0:SHARDS] + found[SHARDS : 2 * SHARDS]
    src = found[2 * SHARDS : 3 * SHARDS] + found[3 * SHARDS :] - 1.0
    ids_ref[...] = ids.astype(I32)
    src_ref[...] = src.astype(I32)
    src_t_ref[...] = jnp.transpose(src).astype(I32)
    for move in moves[3:]:
        move.wait()
    for j in range(BLOCKS):
        pack_ref[DX + j * E : DX + (j + 1) * E, :] = up_ref[:, j * E : (j + 1) * E]


def fetch_kernel(ids_ref, table_ref, out_ref):
    table = table_ref[...].astype(BF)
    cols = jnp.transpose(ids_ref[...].astype(F32))
    lanes = iota((CAP, ROWS), 1).astype(F32)
    for s in range(SHARDS):
        pick = jnp.where(cols[:, s : s + 1] == lanes, 1.0, 0.0).astype(BF)
        out_ref[s] = dot(pick, table).astype(BF)


def arrange(pack_ref, down_ref, up_ref):
    for k in range(TP):
        block = slice(k * RANK, (k + 1) * RANK)
        down_ref[:, block] = pack_ref[k, 0:DX, :]
        for j in range(BLOCKS):
            rows = slice(DX + j * E, DX + (j + 1) * E)
            up_ref[block, j * E : (j + 1) * E] = pack_ref[k, rows, :]


def forward(x, down, up, bias, head, labels):
    hidden = dot(x, down).astype(BF)
    crossed = dot(hidden, up)
    xf = x.astype(F32)
    x_next = xf * (crossed + bias) + xf
    logits = jnp.sum(x_next * head, axis=1, keepdims=True)
    grad_logit = jax.nn.sigmoid(logits) - labels.astype(F32)
    grad_next = grad_logit * head
    return hidden, crossed, xf, x_next, grad_logit, grad_next, grad_next * xf


def quad_row(ref, s):
    parts = [ref[k : k + 1, :].astype(F32) for k in range(QUAD * s, QUAD * (s + 1))]
    return jnp.concatenate(parts, axis=1).astype(I32)


def pool_kernel(rows_ref, src_ref, pack_hbm, pooled_ref, pack_ref, acc_ref, sems):
    moves = [
        pltpu.make_async_copy(pack_hbm.at[k], pack_ref.at[k], sems.at[k]) for k in range(TP)
    ]
    for move in moves:
        move.start()
    bags = iota((BAGS, QUAD * CAP), 0)
    for s in range(SHARDS // QUAD):
        pick = jnp.where(bags == quad_row(src_ref, s), 1.0, 0.0).astype(BF)
        term = dot(pick, rows_ref[s])
        if s == 0:
            acc_ref[...] = term
        else:
            acc_ref[...] += term
    for f in range(F):
        pooled_ref[:, f * E : (f + 1) * E] = acc_ref[f * N : (f + 1) * N, :].astype(BF)
    for move in moves:
        move.wait()


def main_kernel(
    where_ref, pooled_ref, dense_ref, pack_ref, bias_ref, head_ref, label_ref, feedback_ref,
    src_t_ref, carried_ref, send_ref, down_ref, up_ref,
):
    arrange(pack_ref, down_ref, up_ref)
    first = pl.multiple_of(where_ref[0] * N, N)
    x = jnp.concatenate([dense_ref[pl.ds(first, N), :], pooled_ref[...]], axis=1)
    up, bias, head = up_ref[...], bias_ref[...], head_ref[...]
    _, crossed, _, _, _, grad_next, cross = forward(
        x, down_ref[...], up, bias, head, label_ref[pl.ds(first, N), :]
    )
    grad_cross = cross.astype(BF)
    grad_hidden = dot(grad_cross, up, 1, 1).astype(BF)
    back = dot(grad_hidden, down_ref[E:, :], 1, 1)
    carried = grad_next[:, E:] * (crossed[:, E:] + bias[:, E:] + 1.0) + back + feedback_ref[...]
    carried_ref[...] = carried
    sent = carried.astype(BF)
    by_bag = jnp.concatenate([sent[:, f * E : (f + 1) * E] for f in range(F)], axis=0)
    bags = iota((CAP, BAGS), 1)
    for s in range(SHARDS):
        pick = jnp.where(src_t_ref[:, s : s + 1] == bags, 1.0, 0.0).astype(BF)
        send_ref[s] = dot(pick, by_bag).astype(BF)


def grads_kernel(
    where_ref, s0_ref, s1_ref, s2_ref, s3_ref, dense_ref, pack_ref, bias_ref, head_ref, label_ref,
    out_ref, x_ref, hidden_ref, down_grad_ref, up_grad_ref, down_ref, up_ref,
):
    arrange(pack_ref, down_ref, up_ref)
    t = where_ref[0]
    x_ref[:, 0:E] = dense_ref[...]
    for m, ref in enumerate((s0_ref, s1_ref, s2_ref, s3_ref)):
        x_ref[pl.ds(pl.multiple_of((t ^ m) * N, N), N), E:] = ref[...]
    x = x_ref[...]
    hidden, _, _, x_next, grad_logit, _, cross = forward(
        x, down_ref[...], up_ref[...], bias_ref[...], head_ref[...], label_ref[...]
    )
    for k in range(TP):
        hidden_ref[k] = hidden[:, k * RANK : (k + 1) * RANK]
    hidden = hidden_ref[t]
    up = up_ref[pl.ds(pl.multiple_of(t * RANK, RANK), RANK), :]
    grad_cross = cross.astype(BF)
    grad_bias = jnp.sum(cross, axis=0, keepdims=True)
    grad_head = jnp.sum(grad_logit * x_next, axis=0, keepdims=True)
    grad_hidden = dot(grad_cross, up, 1, 1).astype(BF)
    down_grad_ref[...] = dot(x, grad_hidden, 0, 0).astype(BF)
    up_grad_ref[...] = dot(grad_cross, hidden, 0, 0).astype(BF)

    groups = DX // GROUP
    r = iota((groups, DX), 1) - GROUP * iota((groups, DX), 0)
    own = (r >= 0) & (r < GROUP)
    rows = iota((DX, E), 0)
    rest14 = rows - GROUP * jnp.floor((rows.astype(F32) + 0.5) * (1.0 / GROUP)).astype(I32)
    small = jnp.zeros((groups, E), F32)
    for p, v in enumerate((grad_head, grad_bias)):
        spread = jnp.where(own, v, 0.0).astype(BF)
        lanes = jnp.where(iota((DX, E), 1) == rest14 + 16 * p, 1.0, 0.0).astype(BF)
        small = small + dot(spread, lanes)

    block = DP * GROUP
    q = (DP * CHUNK, 2 * block + 32)
    d, rho, col = iota(q, 0) >> 5, iota(q, 0) & 31, iota(q, 1)
    want = jnp.where(
        rho < GROUP,
        GROUP * d + rho,
        jnp.where(
            rho < 2 * GROUP,
            block + GROUP * d + rho - GROUP,
            jnp.where(rho == 2 * GROUP, 2 * block + d, -1),
        ),
    )
    select = jnp.where(col == want, 1.0, 0.0).astype(BF)
    for e in range(SHARDS):
        part = jnp.concatenate([small[DP * e : DP * e + DP], jnp.zeros((24, E), F32)], axis=0)
        block_rows = jnp.concatenate(
            [
                down_grad_ref[block * e : block * (e + 1), :],
                up_grad_ref[block * e : block * (e + 1), :],
                part.astype(BF),
            ],
            axis=0,
        )
        got = dot(select, block_rows).astype(BF)
        for k in range(DP):
            out_ref[k, e] = got[CHUNK * k : CHUNK * (k + 1)]


def scatter_kernel(ids_ref, rows_ref, out_ref, acc_ref):
    rows = iota((ROWS, QUAD * CAP), 0)
    for s in range(SHARDS // QUAD):
        pick = jnp.where(rows == quad_row(ids_ref, s), 1.0, 0.0).astype(BF)
        term = dot(pick, rows_ref[s])
        if s == 0:
            acc_ref[...] = term
        else:
            acc_ref[...] += term
    out_ref[...] = acc_ref[...].astype(BF)


def partner(value, axes, mask):
    size = lax.axis_size(axes)
    return lax.ppermute(value, axes, [(i, i ^ mask) for i in range(size)])


def sds(shape, dtype):
    return jax.ShapeDtypeStruct(shape, dtype)


def local(
    emb_table, row_accum, dense_input, row_shard, local_row, bag_length, labels, feedback,
    cross_down, cross_up, cross_bias, head_weight,
):
    bias, head = cross_bias.reshape(1, DX), head_weight.reshape(1, DX)
    label = labels.reshape(DENSE, 1)
    where = jnp.stack([lax.axis_index(TPA), lax.axis_index("y")]).astype(I32)
    ids, src, src_t, pack = call(
        index_kernel,
        (
            sds((SHARDS, CAP), I32),
            sds((SHARDS, CAP), I32),
            sds((CAP, SHARDS), I32),
            sds((2 * DX, E), BF),
        ),
        (row_shard.transpose(1, 2, 0), local_row.T, bag_length.T, cross_down, cross_up),
        "index",
        scratch=[
            pltpu.VMEM((LOOK, 1, N), I32),
            pltpu.VMEM((LOOK, N), I32),
            pltpu.VMEM((F, N), I32),
            pltpu.VMEM((RANK, DX), BF),
            pltpu.SemaphoreType.DMA((5,)),
        ],
        flops=400_000_000,
        limit=56,
        far=range(5),
    )
    with jax.named_scope("gather_weights"):
        pack_all = lax.all_gather(pack, TPA, axis=0, tiled=False)
    ids = lax.all_to_all(ids, EMB, split_axis=0, concat_axis=0, tiled=True)
    (fetched,) = call(
        fetch_kernel, [sds((SHARDS, CAP, E), BF)], (ids, emb_table), "fetch", flops=1_300_000_000
    )
    returned = lax.all_to_all(fetched, EMB, split_axis=0, concat_axis=0, tiled=True)
    pooled, weights = call(
        pool_kernel,
        [sds((N, POOL), BF), sds((TP, 2 * DX, E), BF)],
        (returned.reshape(SHARDS // QUAD, QUAD * CAP, E), src, pack_all),
        "pool",
        scratch=[
            pltpu.VMEM((BAGS, E), F32),
            pltpu.SemaphoreType.DMA((TP,)),
        ],
        flops=1_060_000_000,
        limit=47,
        far=(2,),
    )
    far = partner(pooled, "xh", 1)
    carried, send = call(
        main_kernel,
        (sds((N, POOL), F32), sds((SHARDS, CAP, E), BF)),
        (where, pooled, dense_input, weights, bias, head, label, feedback, src_t),
        "main",
        scratch=[pltpu.VMEM((DX, TP * RANK), BF), pltpu.VMEM((TP * RANK, DX), BF)],
        flops=10_000_000_000,
        limit=40,
    )
    far, again, send = lax.optimization_barrier((far, pooled, send))
    arrived = lax.all_to_all(send, EMB, split_axis=0, concat_axis=0, tiled=True)

    near, far_near = partner(again, "core", 1), partner(far, "core", 1)
    (part,) = call(
        grads_kernel,
        [sds((DP, SHARDS, CHUNK, E), BF)],
        (where, pooled, near, far, far_near, dense_input, pack_all, bias, head, label),
        "grads",
        scratch=[
            pltpu.VMEM((DENSE, DX), BF),
            pltpu.VMEM((TP, DENSE, RANK), BF),
            pltpu.VMEM((DX, RANK), BF),
            pltpu.VMEM((DX, RANK), BF),
            pltpu.VMEM((DX, TP * RANK), BF),
            pltpu.VMEM((TP * RANK, DX), BF),
        ],
        flops=2_000_000_000,
        limit=40,
    )
    arrived, _ = lax.optimization_barrier((arrived, part))
    over_y = lax.psum_scatter(
        part.reshape(DP * SHARDS * CHUNK, E), "y", scatter_dimension=0, tiled=True
    )
    (row_grad,) = call(
        scatter_kernel,
        [sds((ROWS, E), BF)],
        (ids, arrived.reshape(SHARDS // QUAD, QUAD * CAP, E)),
        "scatter",
        scratch=[pltpu.VMEM((ROWS, E), F32)],
        flops=1_300_000_000,
    )
    owners = ("y", "core")
    pieces = 2 * DP
    by_y = lax.all_to_all(row_grad, owners, split_axis=0, concat_axis=0, tiled=True)
    mine = jnp.sum(by_y.reshape(pieces, ROWS // pieces, E).astype(F32), axis=0)
    mine = (mine + partner(mine, "xh", 1)).astype(BF)
    over_y = over_y.reshape(SHARDS, CHUNK, E)
    over_all = lax.all_to_all(over_y, EMB, split_axis=0, concat_axis=0, tiled=True)
    spread = jnp.broadcast_to(mine[None], (pieces, ROWS // pieces, E)).reshape(ROWS, E)
    spread, over_all = lax.optimization_barrier((spread, over_all))
    full = lax.all_to_all(spread, owners, split_axis=0, concat_axis=0, tiled=True)
    grads = jnp.sum(over_all.astype(F32), axis=0)
    full = full.astype(F32)
    accum_new = row_accum + full * full
    table_new = emb_table - LEARN * full / jnp.sqrt(accum_new)
    grad_down = grads[0:GROUP]
    grad_up = grads[GROUP : 2 * GROUP].T
    grad_head = grads[2 * GROUP, 0:GROUP]
    grad_bias = grads[2 * GROUP, 16 : 16 + GROUP]

    return (table_new, accum_new, carried, grad_down, grad_up, grad_bias, grad_head)


def solution(mesh):
    fine = Mesh(mesh.devices.reshape(2, 8, 8, 2, 2), ("xl", "z", "y", "xh", "core"))
    dense = ("xl", "z", "y")
    every = ("xl", "z", "y", "xh", "core")
    in_specs = (
        P(EMB, None),
        P(EMB, None),
        P(dense, None),
        P(every, None, None),
        P(every, None),
        P(every, None),
        P(dense),
        P(every, None),
        P(None, TPA),
        P(TPA, None),
        P(),
        P(),
    )
    out_specs = (
        P(EMB, None),
        P(EMB, None),
        P(every, None),
        P(dense, TPA),
        P(TPA, dense),
        P(dense),
        P(dense),
    )
    return jax.shard_map(local, mesh=fine, in_specs=in_specs, out_specs=out_specs, check_vma=False)
```

```python
import jax
import jax.numpy as jnp
from jax import lax
from jax.experimental import pallas as pl
from jax.experimental.pallas import tpu as pltpu
from jax.sharding import Mesh, PartitionSpec as P

BF = jnp.bfloat16
F32 = jnp.float32
I32 = jnp.int32
E = 128
F = 13
BAG = 4
LOOK = F * BAG
N = 64
DENSE = 256
TP = 4
DP = 8
SHARDS = 16
CAP = 312
ROWS = 1024
DX = 1792
POOL = F * E
RANK = 128
GROUP = 14
CHUNK = 32
BLOCKS = DX // E
BAGS = N * F
QUAD = 4
LEARN = 0.5
EMB = ("xl", "z")
TPA = ("xh", "core")

VMEM = pl.BlockSpec(memory_space=pltpu.VMEM)
SMEM = pl.BlockSpec(memory_space=pltpu.SMEM)
ANY = pl.BlockSpec(memory_space=pl.ANY)


def iota(shape, axis):
    return lax.broadcasted_iota(I32, shape, axis)


def dot(a, b, ca=1, cb=0):
    return lax.dot_general(a, b, (((ca,), (cb,)), ((), ())), preferred_element_type=F32)


def call(kernel, outs, ins, name, scratch=(), limit=40, flops=0, far=()):
    nbytes = sum(x.size * x.dtype.itemsize for x in ins)
    return pl.pallas_call(
        kernel,
        out_shape=outs,
        in_specs=[SMEM if x.size < 8 else ANY if i in far else VMEM for i, x in enumerate(ins)],
        out_specs=[VMEM] * len(outs),
        scratch_shapes=scratch,
        compiler_params=pltpu.CompilerParams(vmem_limit_bytes=limit << 20),
        cost_estimate=pl.CostEstimate(flops=flops, bytes_accessed=nbytes, transcendentals=0),
        name=name,
    )(*ins)


def index_kernel(
    shard_hbm, row_hbm, len_hbm, down_hbm, up_hbm, ids_ref, src_ref, src_t_ref, pack_ref,
    shard_ref, row_ref, len_ref, up_ref, sems,
):
    moves = [(shard_hbm, shard_ref), (row_hbm, row_ref), (len_hbm, len_ref)]
    moves += [(down_hbm, pack_ref.at[pl.ds(0, DX), :]), (up_hbm, up_ref)]
    moves = [pltpu.make_async_copy(a, b, sems.at[i]) for i, (a, b) in enumerate(moves)]
    for move in moves:
        move.start()
    for move in moves[:3]:
        move.wait()

    def spread(values):
        parts = []
        for j in range(BAG):
            pick = (iota((F, LOOK), 1) == BAG * iota((F, LOOK), 0) + j).astype(F32).astype(BF)
            parts.append(dot(pick, values.astype(F32).astype(BF)))
        return jnp.concatenate(parts, axis=1)

    shard = spread(shard_ref[...].reshape(LOOK, N))
    rows = row_ref[...]
    row_lo, row_hi = spread(rows & 255), spread(rows >> 8)
    lens = len_ref[...].astype(F32)
    lens = jnp.concatenate([lens] * BAG, axis=1)
    wide = (F, BAG * N)
    lane = iota(wide, 1)
    usable = (lane >> 6).astype(F32) < lens
    bag = jnp.where(usable, iota(wide, 0) * N + (lane & (N - 1)) + 1, 0)
    bag_lo, bag_hi = (bag & 255).astype(F32), (bag & ~255).astype(F32)
    row_hi = row_hi * 256.0

    sq = (BAG * N, BAG * N)
    upper = (iota(sq, 0) < iota(sq, 1)).astype(F32).astype(BF)
    shards = iota((SHARDS, BAG * N), 0).astype(F32)
    slots = iota((CAP, BAG * N), 0).astype(F32)
    base = jnp.zeros((SHARDS, 1), F32)
    found = jnp.zeros((4 * SHARDS, CAP), F32)
    for f in range(F):
        hit = shards == shard[f : f + 1, :]
        one = jnp.where(hit, 1.0, 0.0)
        before = dot(one.astype(BF), upper) + base
        base = base + jnp.sum(one, axis=1, keepdims=True)
        rank = jnp.sum(one * before, axis=0, keepdims=True)
        place = jnp.where(slots == rank, 1.0, 0.0).astype(BF)
        values = [
            jnp.where(hit, v[f : f + 1, :], 0.0) for v in (row_lo, row_hi, bag_lo, bag_hi)
        ]
        found = found + dot(jnp.concatenate(values, axis=0).astype(BF), place, 1, 1)
    ids = found[0:SHARDS] + found[SHARDS : 2 * SHARDS]
    src = found[2 * SHARDS : 3 * SHARDS] + found[3 * SHARDS :] - 1.0
    ids_ref[...] = ids.astype(I32)
    src_ref[...] = src.astype(I32)
    src_t_ref[...] = jnp.transpose(src).astype(I32)
    for move in moves[3:]:
        move.wait()
    for j in range(BLOCKS):
        pack_ref[DX + j * E : DX + (j + 1) * E, :] = up_ref[:, j * E : (j + 1) * E]


def fetch_kernel(ids_ref, table_ref, out_ref):
    table = table_ref[...].astype(BF)
    cols = jnp.transpose(ids_ref[...].astype(F32))
    lanes = iota((CAP, ROWS), 1).astype(F32)
    for s in range(SHARDS):
        pick = jnp.where(cols[:, s : s + 1] == lanes, 1.0, 0.0).astype(BF)
        out_ref[s] = dot(pick, table).astype(BF)


def arrange(pack_ref, down_ref, up_ref):
    for k in range(TP):
        block = slice(k * RANK, (k + 1) * RANK)
        down_ref[:, block] = pack_ref[k, 0:DX, :]
        for j in range(BLOCKS):
            rows = slice(DX + j * E, DX + (j + 1) * E)
            up_ref[block, j * E : (j + 1) * E] = pack_ref[k, rows, :]


def forward(x, down, up, bias, head, labels):
    hidden = dot(x, down).astype(BF)
    crossed = dot(hidden, up)
    xf = x.astype(F32)
    x_next = xf * (crossed + bias) + xf
    logits = jnp.sum(x_next * head, axis=1, keepdims=True)
    grad_logit = jax.nn.sigmoid(logits) - labels.astype(F32)
    grad_next = grad_logit * head
    return hidden, crossed, xf, x_next, grad_logit, grad_next, grad_next * xf


def quad_row(ref, s):
    parts = [ref[k : k + 1, :].astype(F32) for k in range(QUAD * s, QUAD * (s + 1))]
    return jnp.concatenate(parts, axis=1).astype(I32)


def pool_kernel(rows_ref, src_ref, pack_hbm, pooled_ref, pack_ref, acc_ref, sems):
    moves = [
        pltpu.make_async_copy(pack_hbm.at[k], pack_ref.at[k], sems.at[k]) for k in range(TP)
    ]
    for move in moves:
        move.start()
    bags = iota((BAGS, QUAD * CAP), 0)
    for s in range(SHARDS // QUAD):
        pick = jnp.where(bags == quad_row(src_ref, s), 1.0, 0.0).astype(BF)
        term = dot(pick, rows_ref[s])
        if s == 0:
            acc_ref[...] = term
        else:
            acc_ref[...] += term
    for f in range(F):
        pooled_ref[:, f * E : (f + 1) * E] = acc_ref[f * N : (f + 1) * N, :].astype(BF)
    for move in moves:
        move.wait()


def main_kernel(
    where_ref, pooled_ref, dense_ref, pack_ref, bias_ref, head_ref, label_ref, feedback_ref,
    src_t_ref, carried_ref, send_ref, down_ref, up_ref,
):
    arrange(pack_ref, down_ref, up_ref)
    first = pl.multiple_of(where_ref[0] * N, N)
    x = jnp.concatenate([dense_ref[pl.ds(first, N), :], pooled_ref[...]], axis=1)
    up, bias, head = up_ref[...], bias_ref[...], head_ref[...]
    _, crossed, _, _, _, grad_next, cross = forward(
        x, down_ref[...], up, bias, head, label_ref[pl.ds(first, N), :]
    )
    grad_cross = cross.astype(BF)
    grad_hidden = dot(grad_cross, up, 1, 1).astype(BF)
    back = dot(grad_hidden, down_ref[E:, :], 1, 1)
    carried = grad_next[:, E:] * (crossed[:, E:] + bias[:, E:] + 1.0) + back + feedback_ref[...]
    carried_ref[...] = carried
    sent = carried.astype(BF)
    by_bag = jnp.concatenate([sent[:, f * E : (f + 1) * E] for f in range(F)], axis=0)
    bags = iota((CAP, BAGS), 1)
    for s in range(SHARDS):
        pick = jnp.where(src_t_ref[:, s : s + 1] == bags, 1.0, 0.0).astype(BF)
        send_ref[s] = dot(pick, by_bag).astype(BF)


def grads_kernel(
    where_ref, s0_ref, s1_ref, s2_ref, s3_ref, dense_ref, pack_ref, bias_ref, head_ref, label_ref,
    out_ref, x_ref, hidden_ref, down_grad_ref, up_grad_ref, down_ref, up_ref,
):
    arrange(pack_ref, down_ref, up_ref)
    t = where_ref[0]
    x_ref[:, 0:E] = dense_ref[...]
    for m, ref in enumerate((s0_ref, s1_ref, s2_ref, s3_ref)):
        x_ref[pl.ds(pl.multiple_of((t ^ m) * N, N), N), E:] = ref[...]
    x = x_ref[...]
    hidden, _, _, x_next, grad_logit, _, cross = forward(
        x, down_ref[...], up_ref[...], bias_ref[...], head_ref[...], label_ref[...]
    )
    for k in range(TP):
        hidden_ref[k] = hidden[:, k * RANK : (k + 1) * RANK]
    hidden = hidden_ref[t]
    up = up_ref[pl.ds(pl.multiple_of(t * RANK, RANK), RANK), :]
    grad_cross = cross.astype(BF)
    grad_bias = jnp.sum(cross, axis=0, keepdims=True)
    grad_head = jnp.sum(grad_logit * x_next, axis=0, keepdims=True)
    grad_hidden = dot(grad_cross, up, 1, 1).astype(BF)
    down_grad_ref[...] = dot(x, grad_hidden, 0, 0).astype(BF)
    up_grad_ref[...] = dot(grad_cross, hidden, 0, 0).astype(BF)

    groups = DX // GROUP
    r = iota((groups, DX), 1) - GROUP * iota((groups, DX), 0)
    own = (r >= 0) & (r < GROUP)
    rows = iota((DX, E), 0)
    rest14 = rows - GROUP * jnp.floor((rows.astype(F32) + 0.5) * (1.0 / GROUP)).astype(I32)
    small = jnp.zeros((groups, E), F32)
    for p, v in enumerate((grad_head, grad_bias)):
        spread = jnp.where(own, v, 0.0).astype(BF)
        lanes = jnp.where(iota((DX, E), 1) == rest14 + 16 * p, 1.0, 0.0).astype(BF)
        small = small + dot(spread, lanes)

    block = DP * GROUP
    q = (DP * CHUNK, 2 * block + 32)
    d, rho, col = iota(q, 0) >> 5, iota(q, 0) & 31, iota(q, 1)
    want = jnp.where(
        rho < GROUP,
        GROUP * d + rho,
        jnp.where(
            rho < 2 * GROUP,
            block + GROUP * d + rho - GROUP,
            jnp.where(rho == 2 * GROUP, 2 * block + d, -1),
        ),
    )
    select = jnp.where(col == want, 1.0, 0.0).astype(BF)
    for e in range(SHARDS):
        part = jnp.concatenate([small[DP * e : DP * e + DP], jnp.zeros((24, E), F32)], axis=0)
        block_rows = jnp.concatenate(
            [
                down_grad_ref[block * e : block * (e + 1), :],
                up_grad_ref[block * e : block * (e + 1), :],
                part.astype(BF),
            ],
            axis=0,
        )
        got = dot(select, block_rows).astype(BF)
        for k in range(DP):
            out_ref[k, e] = got[CHUNK * k : CHUNK * (k + 1)]


def scatter_kernel(ids_ref, rows_ref, out_ref, acc_ref):
    rows = iota((ROWS, QUAD * CAP), 0)
    for s in range(SHARDS // QUAD):
        pick = jnp.where(rows == quad_row(ids_ref, s), 1.0, 0.0).astype(BF)
        term = dot(pick, rows_ref[s])
        if s == 0:
            acc_ref[...] = term
        else:
            acc_ref[...] += term
    out_ref[...] = acc_ref[...].astype(BF)


def partner(value, axes, mask):
    size = lax.axis_size(axes)
    return lax.ppermute(value, axes, [(i, i ^ mask) for i in range(size)])


def sds(shape, dtype):
    return jax.ShapeDtypeStruct(shape, dtype)


def local(
    emb_table, row_accum, dense_input, row_shard, local_row, bag_length, labels, feedback,
    cross_down, cross_up, cross_bias, head_weight,
):
    bias, head = cross_bias.reshape(1, DX), head_weight.reshape(1, DX)
    label = labels.reshape(DENSE, 1)
    where = jnp.stack([lax.axis_index(TPA), lax.axis_index("y")]).astype(I32)
    ids, src, src_t, pack = call(
        index_kernel,
        (
            sds((SHARDS, CAP), I32),
            sds((SHARDS, CAP), I32),
            sds((CAP, SHARDS), I32),
            sds((2 * DX, E), BF),
        ),
        (row_shard.transpose(1, 2, 0), local_row.T, bag_length.T, cross_down, cross_up),
        "index",
        scratch=[
            pltpu.VMEM((LOOK, 1, N), I32),
            pltpu.VMEM((LOOK, N), I32),
            pltpu.VMEM((F, N), I32),
            pltpu.VMEM((RANK, DX), BF),
            pltpu.SemaphoreType.DMA((5,)),
        ],
        flops=400_000_000,
        limit=56,
        far=range(5),
    )
    with jax.named_scope("gather_weights"):
        pack_all = lax.all_gather(pack, TPA, axis=0, tiled=False)
    ids = lax.all_to_all(ids, EMB, split_axis=0, concat_axis=0, tiled=True)
    (fetched,) = call(
        fetch_kernel, [sds((SHARDS, CAP, E), BF)], (ids, emb_table), "fetch", flops=1_300_000_000
    )
    returned = lax.all_to_all(fetched, EMB, split_axis=0, concat_axis=0, tiled=True)
    pooled, weights = call(
        pool_kernel,
        [sds((N, POOL), BF), sds((TP, 2 * DX, E), BF)],
        (returned.reshape(SHARDS // QUAD, QUAD * CAP, E), src, pack_all),
        "pool",
        scratch=[
            pltpu.VMEM((BAGS, E), F32),
            pltpu.SemaphoreType.DMA((TP,)),
        ],
        flops=1_060_000_000,
        limit=47,
        far=(2,),
    )
    far = partner(pooled, "xh", 1)
    carried, send = call(
        main_kernel,
        (sds((N, POOL), F32), sds((SHARDS, CAP, E), BF)),
        (where, pooled, dense_input, weights, bias, head, label, feedback, src_t),
        "main",
        scratch=[pltpu.VMEM((DX, TP * RANK), BF), pltpu.VMEM((TP * RANK, DX), BF)],
        flops=10_000_000_000,
        limit=40,
    )
    far, again, send = lax.optimization_barrier((far, pooled, send))
    arrived = lax.all_to_all(send, EMB, split_axis=0, concat_axis=0, tiled=True)

    near, far_near = partner(again, "core", 1), partner(far, "core", 1)
    (part,) = call(
        grads_kernel,
        [sds((DP, SHARDS, CHUNK, E), BF)],
        (where, pooled, near, far, far_near, dense_input, pack_all, bias, head, label),
        "grads",
        scratch=[
            pltpu.VMEM((DENSE, DX), BF),
            pltpu.VMEM((TP, DENSE, RANK), BF),
            pltpu.VMEM((DX, RANK), BF),
            pltpu.VMEM((DX, RANK), BF),
            pltpu.VMEM((DX, TP * RANK), BF),
            pltpu.VMEM((TP * RANK, DX), BF),
        ],
        flops=2_000_000_000,
        limit=40,
    )
    arrived, _ = lax.optimization_barrier((arrived, part))
    over_y = lax.psum_scatter(
        part.reshape(DP * SHARDS * CHUNK, E), "y", scatter_dimension=0, tiled=True
    )
    (row_grad,) = call(
        scatter_kernel,
        [sds((ROWS, E), BF)],
        (ids, arrived.reshape(SHARDS // QUAD, QUAD * CAP, E)),
        "scatter",
        scratch=[pltpu.VMEM((ROWS, E), F32)],
        flops=1_300_000_000,
    )
    owners = ("y", "core")
    pieces = 2 * DP
    by_y = lax.all_to_all(row_grad, owners, split_axis=0, concat_axis=0, tiled=True)
    mine = jnp.sum(by_y.reshape(pieces, ROWS // pieces, E).astype(F32), axis=0)
    mine = (mine + partner(mine, "xh", 1)).astype(BF)
    over_y = over_y.reshape(SHARDS, CHUNK, E)
    over_all = lax.all_to_all(over_y, EMB, split_axis=0, concat_axis=0, tiled=True)
    near_half = partner(mine, "core", 1)
    lower = lax.axis_index("core") == 0
    mine = jnp.where(
        lower, jnp.stack([mine, near_half]), jnp.stack([near_half, mine])
    ).reshape(ROWS // DP, E)
    spread = jnp.broadcast_to(mine[None], (DP, ROWS // DP, E)).reshape(ROWS, E)
    spread, over_all = lax.optimization_barrier((spread, over_all))
    full = lax.all_to_all(spread, "y", split_axis=0, concat_axis=0, tiled=True)
    grads = jnp.sum(over_all.astype(F32), axis=0)
    full = full.astype(F32)
    accum_new = row_accum + full * full
    table_new = emb_table - LEARN * full / jnp.sqrt(accum_new)
    grad_down = grads[0:GROUP]
    grad_up = grads[GROUP : 2 * GROUP].T
    grad_head = grads[2 * GROUP, 0:GROUP]
    grad_bias = grads[2 * GROUP, 16 : 16 + GROUP]

    return (table_new, accum_new, carried, grad_down, grad_up, grad_bias, grad_head)


def solution(mesh):
    fine = Mesh(mesh.devices.reshape(2, 8, 8, 2, 2), ("xl", "z", "y", "xh", "core"))
    dense = ("xl", "z", "y")
    every = ("xl", "z", "y", "xh", "core")
    in_specs = (
        P(EMB, None),
        P(EMB, None),
        P(dense, None),
        P(every, None, None),
        P(every, None),
        P(every, None),
        P(dense),
        P(every, None),
        P(None, TPA),
        P(TPA, None),
        P(),
        P(),
    )
    out_specs = (
        P(EMB, None),
        P(EMB, None),
        P(every, None),
        P(dense, TPA),
        P(TPA, dense),
        P(dense),
        P(dense),
    )
    return jax.shard_map(local, mesh=fine, in_specs=in_specs, out_specs=out_specs, check_vma=False)
```

```python
import jax
import jax.numpy as jnp
from jax import lax
from jax.experimental import pallas as pl
from jax.experimental.pallas import tpu as pltpu
from jax.sharding import Mesh, PartitionSpec as P

BF = jnp.bfloat16
F32 = jnp.float32
I32 = jnp.int32
E = 128
F = 13
BAG = 4
LOOK = F * BAG
N = 64
DENSE = 256
TP = 4
DP = 8
SHARDS = 16
CAP = 312
ROWS = 1024
DX = 1792
POOL = F * E
RANK = 128
GROUP = 14
CHUNK = 32
BLOCKS = DX // E
BAGS = N * F
QUAD = 4
LEARN = 0.5
EMB = ("xl", "z")
TPA = ("xh", "core")

VMEM = pl.BlockSpec(memory_space=pltpu.VMEM)
SMEM = pl.BlockSpec(memory_space=pltpu.SMEM)
ANY = pl.BlockSpec(memory_space=pl.ANY)


def iota(shape, axis):
    return lax.broadcasted_iota(I32, shape, axis)


def dot(a, b, ca=1, cb=0):
    return lax.dot_general(a, b, (((ca,), (cb,)), ((), ())), preferred_element_type=F32)


def call(kernel, outs, ins, name, scratch=(), limit=40, flops=0, far=()):
    nbytes = sum(x.size * x.dtype.itemsize for x in ins)
    return pl.pallas_call(
        kernel,
        out_shape=outs,
        in_specs=[SMEM if x.size < 8 else ANY if i in far else VMEM for i, x in enumerate(ins)],
        out_specs=[VMEM] * len(outs),
        scratch_shapes=scratch,
        compiler_params=pltpu.CompilerParams(vmem_limit_bytes=limit << 20),
        cost_estimate=pl.CostEstimate(flops=flops, bytes_accessed=nbytes, transcendentals=0),
        name=name,
    )(*ins)


def index_kernel(
    shard_hbm, row_hbm, len_hbm, down_hbm, up_hbm, ids_ref, src_ref, src_t_ref, pack_ref,
    shard_ref, row_ref, len_ref, up_ref, sems,
):
    moves = [(shard_hbm, shard_ref), (row_hbm, row_ref), (len_hbm, len_ref)]
    moves += [(down_hbm, pack_ref.at[pl.ds(0, DX), :]), (up_hbm, up_ref)]
    moves = [pltpu.make_async_copy(a, b, sems.at[i]) for i, (a, b) in enumerate(moves)]
    for move in moves:
        move.start()
    for move in moves[:3]:
        move.wait()

    def spread(values):
        parts = []
        for j in range(BAG):
            pick = (iota((F, LOOK), 1) == BAG * iota((F, LOOK), 0) + j).astype(F32).astype(BF)
            parts.append(dot(pick, values.astype(F32).astype(BF)))
        return jnp.concatenate(parts, axis=1)

    shard = spread(shard_ref[...].reshape(LOOK, N))
    rows = row_ref[...]
    row_lo, row_hi = spread(rows & 255), spread(rows >> 8)
    lens = len_ref[...].astype(F32)
    lens = jnp.concatenate([lens] * BAG, axis=1)
    wide = (F, BAG * N)
    lane = iota(wide, 1)
    usable = (lane >> 6).astype(F32) < lens
    bag = jnp.where(usable, iota(wide, 0) * N + (lane & (N - 1)) + 1, 0)
    bag_lo, bag_hi = (bag & 255).astype(F32), (bag & ~255).astype(F32)
    row_hi = row_hi * 256.0

    sq = (BAG * N, BAG * N)
    upper = (iota(sq, 0) < iota(sq, 1)).astype(F32).astype(BF)
    shards = iota((SHARDS, BAG * N), 0).astype(F32)
    slots = iota((CAP, BAG * N), 0).astype(F32)
    base = jnp.zeros((SHARDS, 1), F32)
    found = jnp.zeros((4 * SHARDS, CAP), F32)
    for f in range(F):
        hit = shards == shard[f : f + 1, :]
        one = jnp.where(hit, 1.0, 0.0)
        before = dot(one.astype(BF), upper) + base
        base = base + jnp.sum(one, axis=1, keepdims=True)
        rank = jnp.sum(one * before, axis=0, keepdims=True)
        place = jnp.where(slots == rank, 1.0, 0.0).astype(BF)
        values = [
            jnp.where(hit, v[f : f + 1, :], 0.0) for v in (row_lo, row_hi, bag_lo, bag_hi)
        ]
        found = found + dot(jnp.concatenate(values, axis=0).astype(BF), place, 1, 1)
    ids = found[0:SHARDS] + found[SHARDS : 2 * SHARDS]
    src = found[2 * SHARDS : 3 * SHARDS] + found[3 * SHARDS :] - 1.0
    ids = ids.astype(I32)
    for s in range(SHARDS):
        ids_ref[s] = ids[s : s + 1, :]
    src_ref[...] = src.astype(I32)
    src_t_ref[...] = jnp.transpose(src).astype(I32)
    for move in moves[3:]:
        move.wait()
    for j in range(BLOCKS):
        pack_ref[DX + j * E : DX + (j + 1) * E, :] = up_ref[:, j * E : (j + 1) * E]


def fetch_kernel(ids_ref, table_ref, out_ref):
    table = table_ref[...].astype(BF)
    cols = jnp.transpose(ids_ref[...].astype(F32))
    lanes = iota((CAP, ROWS), 1).astype(F32)
    for s in range(SHARDS):
        pick = jnp.where(cols[:, s : s + 1] == lanes, 1.0, 0.0).astype(BF)
        out_ref[s] = dot(pick, table).astype(BF)


def arrange(pack_ref, down_ref, up_ref):
    for k in range(TP):
        block = slice(k * RANK, (k + 1) * RANK)
        down_ref[:, block] = pack_ref[k, 0:DX, :]
        for j in range(BLOCKS):
            rows = slice(DX + j * E, DX + (j + 1) * E)
            up_ref[block, j * E : (j + 1) * E] = pack_ref[k, rows, :]


def forward(x, down, up, bias, head, labels):
    hidden = dot(x, down).astype(BF)
    crossed = dot(hidden, up)
    xf = x.astype(F32)
    x_next = xf * (crossed + bias) + xf
    logits = jnp.sum(x_next * head, axis=1, keepdims=True)
    grad_logit = jax.nn.sigmoid(logits) - labels.astype(F32)
    grad_next = grad_logit * head
    return hidden, crossed, xf, x_next, grad_logit, grad_next, grad_next * xf


def quad_row(ref, s):
    parts = [ref[k : k + 1, :].astype(F32) for k in range(QUAD * s, QUAD * (s + 1))]
    return jnp.concatenate(parts, axis=1).astype(I32)


def pool_kernel(rows_ref, src_ref, pack_hbm, pooled_ref, pack_ref, acc_ref, sems):
    moves = [
        pltpu.make_async_copy(pack_hbm.at[k], pack_ref.at[k], sems.at[k]) for k in range(TP)
    ]
    for move in moves:
        move.start()
    bags = iota((BAGS, QUAD * CAP), 0)
    for s in range(SHARDS // QUAD):
        pick = jnp.where(bags == quad_row(src_ref, s), 1.0, 0.0).astype(BF)
        term = dot(pick, rows_ref[s])
        if s == 0:
            acc_ref[...] = term
        else:
            acc_ref[...] += term
    for f in range(F):
        pooled_ref[:, f * E : (f + 1) * E] = acc_ref[f * N : (f + 1) * N, :].astype(BF)
    for move in moves:
        move.wait()


def main_kernel(
    where_ref, pooled_ref, dense_ref, pack_ref, bias_ref, head_ref, label_ref, feedback_ref,
    src_t_ref, carried_ref, send_ref, down_ref, up_ref,
):
    arrange(pack_ref, down_ref, up_ref)
    first = pl.multiple_of(where_ref[0] * N, N)
    x = jnp.concatenate([dense_ref[pl.ds(first, N), :], pooled_ref[...]], axis=1)
    up, bias, head = up_ref[...], bias_ref[...], head_ref[...]
    _, crossed, _, _, _, grad_next, cross = forward(
        x, down_ref[...], up, bias, head, label_ref[pl.ds(first, N), :]
    )
    grad_cross = cross.astype(BF)
    grad_hidden = dot(grad_cross, up, 1, 1).astype(BF)
    back = dot(grad_hidden, down_ref[E:, :], 1, 1)
    carried = grad_next[:, E:] * (crossed[:, E:] + bias[:, E:] + 1.0) + back + feedback_ref[...]
    carried_ref[...] = carried
    sent = carried.astype(BF)
    by_bag = jnp.concatenate([sent[:, f * E : (f + 1) * E] for f in range(F)], axis=0)
    bags = iota((CAP, BAGS), 1)
    for s in range(SHARDS):
        pick = jnp.where(src_t_ref[:, s : s + 1] == bags, 1.0, 0.0).astype(BF)
        send_ref[s] = dot(pick, by_bag).astype(BF)


def grads_kernel(
    where_ref, s0_ref, s1_ref, s2_ref, s3_ref, dense_ref, pack_ref, bias_ref, head_ref, label_ref,
    out_ref, x_ref, hidden_ref, down_grad_ref, up_grad_ref, down_ref, up_ref,
):
    arrange(pack_ref, down_ref, up_ref)
    t = where_ref[0]
    x_ref[:, 0:E] = dense_ref[...]
    for m, ref in enumerate((s0_ref, s1_ref, s2_ref, s3_ref)):
        x_ref[pl.ds(pl.multiple_of((t ^ m) * N, N), N), E:] = ref[...]
    x = x_ref[...]
    hidden, _, _, x_next, grad_logit, _, cross = forward(
        x, down_ref[...], up_ref[...], bias_ref[...], head_ref[...], label_ref[...]
    )
    for k in range(TP):
        hidden_ref[k] = hidden[:, k * RANK : (k + 1) * RANK]
    hidden = hidden_ref[t]
    up = up_ref[pl.ds(pl.multiple_of(t * RANK, RANK), RANK), :]
    grad_cross = cross.astype(BF)
    grad_bias = jnp.sum(cross, axis=0, keepdims=True)
    grad_head = jnp.sum(grad_logit * x_next, axis=0, keepdims=True)
    grad_hidden = dot(grad_cross, up, 1, 1).astype(BF)
    down_grad_ref[...] = dot(x, grad_hidden, 0, 0).astype(BF)
    up_grad_ref[...] = dot(grad_cross, hidden, 0, 0).astype(BF)

    groups = DX // GROUP
    r = iota((groups, DX), 1) - GROUP * iota((groups, DX), 0)
    own = (r >= 0) & (r < GROUP)
    rows = iota((DX, E), 0)
    rest14 = rows - GROUP * jnp.floor((rows.astype(F32) + 0.5) * (1.0 / GROUP)).astype(I32)
    small = jnp.zeros((groups, E), F32)
    for p, v in enumerate((grad_head, grad_bias)):
        spread = jnp.where(own, v, 0.0).astype(BF)
        lanes = jnp.where(iota((DX, E), 1) == rest14 + 16 * p, 1.0, 0.0).astype(BF)
        small = small + dot(spread, lanes)

    block = DP * GROUP
    q = (DP * CHUNK, 2 * block + 32)
    d, rho, col = iota(q, 0) >> 5, iota(q, 0) & 31, iota(q, 1)
    want = jnp.where(
        rho < GROUP,
        GROUP * d + rho,
        jnp.where(
            rho < 2 * GROUP,
            block + GROUP * d + rho - GROUP,
            jnp.where(rho == 2 * GROUP, 2 * block + d, -1),
        ),
    )
    select = jnp.where(col == want, 1.0, 0.0).astype(BF)
    for e in range(SHARDS):
        part = jnp.concatenate([small[DP * e : DP * e + DP], jnp.zeros((24, E), F32)], axis=0)
        block_rows = jnp.concatenate(
            [
                down_grad_ref[block * e : block * (e + 1), :],
                up_grad_ref[block * e : block * (e + 1), :],
                part.astype(BF),
            ],
            axis=0,
        )
        got = dot(select, block_rows).astype(BF)
        for k in range(DP):
            out_ref[k, e] = got[CHUNK * k : CHUNK * (k + 1)]


def scatter_kernel(ids_ref, rows_ref, out_ref, acc_ref):
    rows = iota((ROWS, QUAD * CAP), 0)
    for s in range(SHARDS // QUAD):
        pick = jnp.where(rows == quad_row(ids_ref, s), 1.0, 0.0).astype(BF)
        term = dot(pick, rows_ref[s])
        if s == 0:
            acc_ref[...] = term
        else:
            acc_ref[...] += term
    out_ref[...] = acc_ref[...].astype(BF)


def partner(value, axes, mask):
    size = lax.axis_size(axes)
    return lax.ppermute(value, axes, [(i, i ^ mask) for i in range(size)])


def sds(shape, dtype):
    return jax.ShapeDtypeStruct(shape, dtype)


def local(
    emb_table, row_accum, dense_input, row_shard, local_row, bag_length, labels, feedback,
    cross_down, cross_up, cross_bias, head_weight,
):
    bias, head = cross_bias.reshape(1, DX), head_weight.reshape(1, DX)
    label = labels.reshape(DENSE, 1)
    where = jnp.stack([lax.axis_index(TPA), lax.axis_index("y")]).astype(I32)
    ids, src, src_t, pack = call(
        index_kernel,
        (
            sds((SHARDS, 1, CAP), I32),
            sds((SHARDS, CAP), I32),
            sds((CAP, SHARDS), I32),
            sds((2 * DX, E), BF),
        ),
        (row_shard.transpose(1, 2, 0), local_row.T, bag_length.T, cross_down, cross_up),
        "index",
        scratch=[
            pltpu.VMEM((LOOK, 1, N), I32),
            pltpu.VMEM((LOOK, N), I32),
            pltpu.VMEM((F, N), I32),
            pltpu.VMEM((RANK, DX), BF),
            pltpu.SemaphoreType.DMA((5,)),
        ],
        flops=400_000_000,
        limit=56,
        far=range(5),
    )
    with jax.named_scope("gather_weights"):
        pack_all = lax.all_gather(pack, TPA, axis=0, tiled=False)
    ids = lax.all_to_all(ids, EMB, split_axis=0, concat_axis=0, tiled=True)
    ids = ids.reshape(SHARDS, CAP)
    (fetched,) = call(
        fetch_kernel, [sds((SHARDS, CAP, E), BF)], (ids, emb_table), "fetch", flops=1_300_000_000
    )
    returned = lax.all_to_all(fetched, EMB, split_axis=0, concat_axis=0, tiled=True)
    pooled, weights = call(
        pool_kernel,
        [sds((N, POOL), BF), sds((TP, 2 * DX, E), BF)],
        (returned.reshape(SHARDS // QUAD, QUAD * CAP, E), src, pack_all),
        "pool",
        scratch=[
            pltpu.VMEM((BAGS, E), F32),
            pltpu.SemaphoreType.DMA((TP,)),
        ],
        flops=1_060_000_000,
        limit=47,
        far=(2,),
    )
    far = partner(pooled, "xh", 1)
    carried, send = call(
        main_kernel,
        (sds((N, POOL), F32), sds((SHARDS, CAP, E), BF)),
        (where, pooled, dense_input, weights, bias, head, label, feedback, src_t),
        "main",
        scratch=[pltpu.VMEM((DX, TP * RANK), BF), pltpu.VMEM((TP * RANK, DX), BF)],
        flops=10_000_000_000,
        limit=40,
    )
    far, again, send = lax.optimization_barrier((far, pooled, send))
    arrived = lax.all_to_all(send, EMB, split_axis=0, concat_axis=0, tiled=True)

    near, far_near = partner(again, "core", 1), partner(far, "core", 1)
    (part,) = call(
        grads_kernel,
        [sds((DP, SHARDS, CHUNK, E), BF)],
        (where, pooled, near, far, far_near, dense_input, pack_all, bias, head, label),
        "grads",
        scratch=[
            pltpu.VMEM((DENSE, DX), BF),
            pltpu.VMEM((TP, DENSE, RANK), BF),
            pltpu.VMEM((DX, RANK), BF),
            pltpu.VMEM((DX, RANK), BF),
            pltpu.VMEM((DX, TP * RANK), BF),
            pltpu.VMEM((TP * RANK, DX), BF),
        ],
        flops=2_000_000_000,
        limit=40,
    )
    arrived, _ = lax.optimization_barrier((arrived, part))
    over_y = lax.psum_scatter(
        part.reshape(DP * SHARDS * CHUNK, E), "y", scatter_dimension=0, tiled=True
    )
    (row_grad,) = call(
        scatter_kernel,
        [sds((ROWS, E), BF)],
        (ids, arrived.reshape(SHARDS // QUAD, QUAD * CAP, E)),
        "scatter",
        scratch=[pltpu.VMEM((ROWS, E), F32)],
        flops=1_300_000_000,
    )
    owners = ("y", "core")
    pieces = 2 * DP
    by_y = lax.all_to_all(row_grad, owners, split_axis=0, concat_axis=0, tiled=True)
    mine = jnp.sum(by_y.reshape(pieces, ROWS // pieces, E).astype(F32), axis=0)
    mine = (mine + partner(mine, "xh", 1)).astype(BF)
    over_y = over_y.reshape(SHARDS, CHUNK, E)
    over_all = lax.all_to_all(over_y, EMB, split_axis=0, concat_axis=0, tiled=True)
    near_half = partner(mine, "core", 1)
    lower = lax.axis_index("core") == 0
    mine = jnp.where(
        lower, jnp.stack([mine, near_half]), jnp.stack([near_half, mine])
    ).reshape(ROWS // DP, E)
    spread = jnp.broadcast_to(mine[None], (DP, ROWS // DP, E)).reshape(ROWS, E)
    spread, over_all = lax.optimization_barrier((spread, over_all))
    full = lax.all_to_all(spread, "y", split_axis=0, concat_axis=0, tiled=True)
    grads = jnp.sum(over_all.astype(F32), axis=0)
    full = full.astype(F32)
    accum_new = row_accum + full * full
    table_new = emb_table - LEARN * full / jnp.sqrt(accum_new)
    grad_down = grads[0:GROUP]
    grad_up = grads[GROUP : 2 * GROUP].T
    grad_head = grads[2 * GROUP, 0:GROUP]
    grad_bias = grads[2 * GROUP, 16 : 16 + GROUP]

    return (table_new, accum_new, carried, grad_down, grad_up, grad_bias, grad_head)


def solution(mesh):
    fine = Mesh(mesh.devices.reshape(2, 8, 8, 2, 2), ("xl", "z", "y", "xh", "core"))
    dense = ("xl", "z", "y")
    every = ("xl", "z", "y", "xh", "core")
    in_specs = (
        P(EMB, None),
        P(EMB, None),
        P(dense, None),
        P(every, None, None),
        P(every, None),
        P(every, None),
        P(dense),
        P(every, None),
        P(None, TPA),
        P(TPA, None),
        P(),
        P(),
    )
    out_specs = (
        P(EMB, None),
        P(EMB, None),
        P(every, None),
        P(dense, TPA),
        P(TPA, dense),
        P(dense),
        P(dense),
    )
    return jax.shard_map(local, mesh=fine, in_specs=in_specs, out_specs=out_specs, check_vma=False)
```
